128 devices in a mesh: rows: 4 (over y), cols: 32 (over z, x, core).
Axes of the slice: x: 4, y: 4, z: 4, core: 2. Of those that a mesh axis runs over, the one named last changes fastest.
Arguments:
- sigma_in: bfloat16 [2048, 32768], P('rows', 'cols'), may hold values from -6 to 6
- theta_in: bfloat16 [2048, 32768], P('rows', 'cols'), may hold values from -6 to 6
- var_rows: float32 [2048], P('rows'), may hold values from 0.3 to 3
- var_cols: float32 [32768], P('cols'), may hold values from 0.3 to 3
- row_nbrs: int32 [8, 3], replicated, may hold values from 0 to 7, as said below
- row_vals: bfloat16 [8, 3, 256, 256], replicated, may hold values from -0.21875 to 0.21875
- col_nbrs: int32 [128, 20], replicated, may hold values from 0 to 127, as said below
- col_vals: bfloat16 [128, 20, 256, 256], P('cols'), may hold values from -0.078125 to 0.078125
Outputs:
- nngp_out: float32 [2048, 32768], P('rows', 'cols')
- ntk_out: float32 [2048, 32768], P('rows', 'cols')
The draws below stay inside these ranges and needn't reach their ends.
Inputs may be any that keep to these rules, and one draw needn't show every extreme that they name: `row_nbrs`: the 3 entries of one row are distinct. `col_nbrs`: column block c belongs to index c // 4 of cols. The lists of the 4 column blocks of one index of cols name, of each other index of cols, at most one block (possibly several times).
All inputs are finite; a program needn't handle non-finite values.
Results may differ from the reference program's by a relative error of at most 0.0026.
Values may be sent and summed in bfloat16 or wider, within the bound.
A program may use at most 256 MiB of HBM per device.

```python
import math
import jax
import jax.numpy as jnp
from jax import lax

BLK = 256
PB_DEV = 2
CB_DEV = 4
KL = 3
KR = 20
NPB = 8
PANEL = 2048
NCB = 128
NODES = 32768
PEERS = 20
N_ROWS = 4
N_COLS = 32


def draw_row_nbrs(key, part):
    key = jax.random.fold_in(key, 11)
    subkeys = jax.random.split(key, PB_DEV * N_ROWS)

    def per_block(subkey):
        return jax.random.permutation(subkey, PB_DEV * N_ROWS)[:KL]
    return jax.vmap(per_block)(subkeys).astype(jnp.int32)


def draw_col_nbrs(key, part):
    key = jax.random.fold_in(key, 23)
    subkeys = jax.random.split(key, N_COLS)

    def per_target(target, subkey):
        first_key, second_key, third_key = jax.random.split(subkey, 3)
        offsets = jax.random.permutation(first_key, N_COLS - 1)[:PEERS] + 1
        peer_ids = (target + offsets) % N_COLS
        peer_blocks = jax.random.randint(second_key, (PEERS,), 0, CB_DEV)
        candidates = jnp.concatenate([target * CB_DEV + jnp.arange(CB_DEV), peer_ids * CB_DEV + peer_blocks])
        slot_picks = jax.random.randint(third_key, (CB_DEV, KR), 0, CB_DEV + PEERS)
        return candidates[slot_picks]
    listed = jax.vmap(per_target)(jnp.arange(N_COLS), subkeys)
    return listed.reshape(CB_DEV * N_COLS, KR).astype(jnp.int32)


def shard_levels(own_key, shape, cuts, least, largest):
    def one(axis_at, parts):
        heights = jax.random.uniform(jax.random.fold_in(jax.random.fold_in(own_key, 6), axis_at), (parts,), jnp.float32, least / len(cuts), largest / len(cuts))
        return jnp.repeat(jnp.exp(heights), shape[axis_at] // parts).reshape((-1,) + (1,) * (len(shape) - axis_at - 1))

    factor_of = one(*cuts[0])
    for cut in cuts[1:]:
        factor_of = factor_of * one(*cut)
    return factor_of


def noise(rng, shape, spread, reach, pieces=(), held_as=jnp.bfloat16):
    level = shard_levels(rng, shape, pieces, -0.22, 0.18) if pieces else 1.0
    result = jax.random.normal(rng, shape, jnp.float32) * spread * level
    return jnp.minimum(jnp.maximum(result, -reach), reach).astype(held_as)


def setup_inputs(seed: int = 0) -> dict:
    seeds = jax.random.split(jax.random.key(seed), 9)
    return {
        "sigma_in": noise(seeds[0], (PANEL, NODES), 1.0, 6.0, ((0, 4), (1, 32))),
        "theta_in": noise(seeds[1], (PANEL, NODES), 1.0, 6.0, ((0, 4), (1, 32))),
        "var_rows": jnp.clip(jnp.exp(math.log(3.0) - 2.3025851 * jax.random.uniform(seeds[2], (PANEL,), jnp.float32) ** shard_levels(seeds[2], (PANEL,), ((0, 4),), -0.2, 0.2)), 0.3, 3.0),
        "var_cols": jnp.clip(jnp.exp(math.log(3.0) - 2.3025851 * jax.random.uniform(seeds[3], (NODES,), jnp.float32) ** shard_levels(seeds[3], (NODES,), ((0, 32),), -0.2, 0.2)), 0.3, 3.0),
        "row_nbrs": draw_row_nbrs(jax.random.fold_in(seeds[8], 71), 0),
        "row_vals": noise(seeds[5], (NPB, KL, BLK, BLK), (KL * BLK) ** -0.5, 0.21875),
        "col_nbrs": draw_col_nbrs(jax.random.fold_in(seeds[8], 71), 0),
        "col_vals": noise(seeds[7], (NCB, KR, BLK, BLK), (KR * BLK) ** -0.5, 0.078125, ((0, 32),)),
    }


def reference(sigma_in, theta_in, var_rows, var_cols, row_nbrs, row_vals, col_nbrs, col_vals):
    block_size = row_vals.shape[2]
    panel_blocks = row_nbrs.shape[0]
    panel_rows = sigma_in.shape[0]
    node_count = sigma_in.shape[1]
    col_blocks = col_nbrs.shape[0]
    sigma_blocks = sigma_in.astype(jnp.float32).reshape(panel_blocks, block_size, node_count)
    theta_blocks = theta_in.astype(jnp.float32).reshape(panel_blocks, block_size, node_count)

    def left_block(inputs):
        neighbours, values = inputs
        weights = values.astype(jnp.float32)
        left_sigma = jnp.einsum('kij,kjn->in', weights, sigma_blocks[neighbours])
        left_theta = jnp.einsum('kij,kjn->in', weights, theta_blocks[neighbours])
        return (left_sigma, left_theta)
    part_sigma, part_theta = lax.map(left_block, (row_nbrs, row_vals))
    panel_sigma = part_sigma.reshape(panel_rows, node_count).astype(jnp.bfloat16)
    panel_theta = part_theta.reshape(panel_rows, node_count).astype(jnp.bfloat16)
    sigma_cols = panel_sigma.astype(jnp.float32).reshape(panel_rows, col_blocks, block_size)
    theta_cols = panel_theta.astype(jnp.float32).reshape(panel_rows, col_blocks, block_size)

    def right_block(inputs):
        neighbours, values = inputs
        weights = values.astype(jnp.float32)
        right_sigma = jnp.einsum('rkj,kij->ri', sigma_cols[:, neighbours, :], weights)
        right_theta = jnp.einsum('rkj,kij->ri', theta_cols[:, neighbours, :], weights)
        return (right_sigma, right_theta)
    out_sigma, out_theta = lax.map(right_block, (col_nbrs, col_vals))
    agg_sigma = jnp.transpose(out_sigma, (1, 0, 2)).reshape(panel_rows, node_count)
    agg_theta = jnp.transpose(out_theta, (1, 0, 2)).reshape(panel_rows, node_count)
    scale_rc = jnp.sqrt(var_rows[:, None] * var_cols[None, :])
    hypotenuse = jnp.sqrt(scale_rc * scale_rc + agg_sigma * agg_sigma)
    correlation = agg_sigma / hypotenuse
    arc_angle = jnp.arccos(correlation)
    nngp_out = scale_rc / jnp.pi * (scale_rc / hypotenuse + (jnp.pi - arc_angle) * correlation)
    ntk_out = nngp_out + agg_theta * (jnp.pi - arc_angle) / jnp.pi
    return (nngp_out, ntk_out)
```

```python
import functools
import math

import jax
import jax.numpy as jnp
from jax import lax
from jax.experimental import pallas as pl
from jax.experimental.pallas import tpu as pltpu
from jax.sharding import PartitionSpec as P

MESH = pl.DeviceIdType.MESH
BF16 = jnp.bfloat16
F32 = jnp.float32

ATAN = (
    0.9999998979,
    -0.3333196033,
    0.1996924122,
    -0.1401660921,
    0.09906147193,
    -0.05936764426,
    0.02416647519,
    -0.004668829048,
)


def arc(t):
    t2 = t * t
    total = jnp.full_like(t, ATAN[-1])
    for c in ATAN[-2::-1]:
        total = total * t2 + c
    return total * t


def kernel(
    want, index, row_nbrs, theta, sigma, var_rows, var_cols, row_vals, col_vals,
    nngp, ntk,
    weights, row_weights, gathered_s, gathered_t, agg_theta, out_n, out_k,
    pa0, pa1, pa2, pa3, pb0, pb1, pb2, pb3,
    ra0, ra1, ra2, ra3, rb0, rb1, rb2, rb3,
    sa0, sa1, sb0, sb1,
    w_sem, rv_sem, own_sem, ys_send, ys_recv, yt_send, yt_recv,
    one_send, one_recv, two_send, two_recv, out_sem,
):
    pools = ((pa0, pb0), (pa1, pb1), (pa2, pb2), (pa3, pb3))
    slots = ((ra0, rb0), (ra1, rb1), (ra2, rb2), (ra3, rb3))
    sends = ((sa0, sb0), (sa1, sb1), (sa0, sb0), (sa1, sb1))
    y = lax.axis_index("rows")
    col = lax.axis_index("cols")
    z, x, core = col // 8, (col // 2) % 4, col % 2

    def at(dy, dz, dx, dc):
        return (
            lax.rem(y + dy, 4),
            (lax.rem(z + dz, 4) * 4 + lax.rem(x + dx, 4)) * 2 + lax.rem(core + dc, 2),
        )

    loads = []

    def load(src, dst, sem):
        copy = pltpu.make_async_copy(src, dst, sem)
        copy.start()
        loads.append(copy)
        return copy

    own_pool = {}
    for ph in range(2):
        for st in range(2):
            rows = pl.ds(ph * 256 + st * 128, 128)
            own_pool[ph, st] = [
                load(theta.at[rows, pl.ds(b * 256, 256)], pools[ph][st].at[(z, x)[st], b], own_sem.at[ph, st, b])
                for b in range(4)
            ]
    own_s = []
    for half in range(2):
        own_s.append(load(sigma.at[pl.ds(half * 256, 256)], gathered_s.at[2 * y + half], own_sem.at[2, half, 0]))

    barrier = pltpu.get_barrier_semaphore()
    partners = [(dy, 0, 0, 0) for dy in (1, 2, 3)]
    partners += [(0, dz, 0, dc) for dz in (1, 2, 3) for dc in (0, 1)]
    partners += [(0, 0, dx, dc) for dx in (1, 2, 3) for dc in (0, 1)]
    partners += [(0, 0, 0, 1)]
    for p in partners:
        pl.semaphore_signal(barrier, inc=1, device_id=at(*p), device_id_type=MESH)
    pl.semaphore_wait(barrier, len(partners))

    def line(st, d, dc):
        return at(0, d, 0, dc) if st == 0 else at(0, 0, d, dc)

    def remote(src, dst, ssem, rsem, device):
        copy = pltpu.make_async_remote_copy(
            src_ref=src, dst_ref=dst, send_sem=ssem, recv_sem=rsem, device_id=device, device_id_type=MESH
        )
        copy.start()
        return copy

    first = {}

    def stage_one(ph):
        for d in (1, 3, 2):
            for st in range(2):
                mine = (z, x)[st]
                first[ph, st, d] = remote(
                    pools[ph][st].at[mine],
                    pools[ph][st].at[mine],
                    one_send.at[ph, st, d - 1],
                    one_recv.at[ph, st, d - 1],
                    line(st, d, 0),
                )

    second = {}

    def stage_two(ph):
        for st in range(2):
            for d in (1, 2, 3):
                first[ph, st, d].wait_recv()
        for st in range(2):
            pool, out, here = pools[ph][st], sends[ph][st], slots[ph][st]
            place = (x if st == 0 else z) * 2 + core

            def source_at(s):
                return ((s * 4 + x) if st == 0 else (z * 4 + s)) * 2 + core

            if ph >= 2:
                for j in range(1, 8):
                    second[ph - 2, st, j].wait_send()

            def pack(i, carry):
                j, s = i // 4 + 1, i % 4
                d, dc = j // 2, j % 2
                other = line(1 - st, d, dc)[1]
                block = want[other * 32 + source_at(s)]
                out[j - 1, s] = pool[s, block]
                return carry

            lax.fori_loop(0, 28, pack, 0)
            for j in (2, 3, 6, 7, 4, 5, 1):
                second[ph, st, j] = remote(
                    out.at[j - 1],
                    here.at[pl.ds(place * 4, 4)],
                    two_send.at[ph, st, j - 1],
                    two_recv.at[ph, st, j - 1],
                    line(1 - st, j // 2, j % 2),
                )
        for st in range(2):
            pool, here = pools[ph][st], slots[ph][st]
            place = (x if st == 0 else z) * 2 + core
            for s in range(4):
                src = ((s * 4 + x) if st == 0 else (z * 4 + s)) * 2 + core
                block = want[col * 32 + src]
                here[place * 4 + s] = pool[s, block]
            for b in range(4):
                here[32 + b] = pool[(z, x)[st], b]

    def arrived(ph):
        for st in range(2):
            for j in range(1, 8):
                second[ph, st, j].wait_recv()

    def right(ph, c):
        here_a, here_b = slots[ph]
        total = None
        for k in range(20):
            e = c * 20 + k
            lhs = jnp.concatenate([here_a[index[e]], here_b[index[80 + e]]], axis=0)
            part = lax.dot_general(lhs, weights[e], (((1,), (1,)), ((), ())), preferred_element_type=F32)
            total = part if total is None else total + part
        return total

    def left(gathered, p):
        total = None
        for k in range(3):
            n = row_nbrs[(2 * y + p) * 3 + k]
            part = jnp.dot(row_weights[p * 3 + k], gathered[n], preferred_element_type=F32)
            total = part if total is None else total + part
        return total

    for ph in range(2):
        for st in range(2):
            for copy in own_pool[ph, st]:
                copy.wait()
        stage_one(ph)
    ys = [
        remote(
            sigma.at[pl.ds(half * 256, 256)],
            gathered_s.at[2 * y + half],
            ys_send.at[half, d - 1],
            ys_recv.at[half, d - 1],
            at(d, 0, 0, 0),
        )
        for half in range(2)
        for d in (1, 3, 2)
    ]
    w_load = [load(col_vals.at[c], weights.at[pl.ds(c * 20, 20)], w_sem.at[c]) for c in range(4)]
    rv_load = [load(row_vals.at[2 * y + p], row_weights.at[pl.ds(p * 3, 3)], rv_sem.at[p]) for p in range(2)]

    stage_two(0)
    stage_two(1)

    for copy in own_s + rv_load:
        copy.wait()
    for copy in ys:
        copy.wait_recv()
    for p in range(2):

        total = left(gathered_s, p).astype(BF16)
        ph = 2 + p
        for st in range(2):
            for b in range(4):
                pools[ph][st][(z, x)[st], b] = total[st * 128 : (st + 1) * 128, b * 256 : (b + 1) * 256]
        stage_one(ph)

    yt = []
    for copy in w_load:
        copy.wait()
    for half in range(2):
        arrived(half)

        def right_t(c, carry, half=half):
            cols = pl.ds(pl.multiple_of(c * 256, 256), 256)
            gathered_t[2 * y + half, :, cols] = right(half, c).astype(BF16)
            return carry

        lax.fori_loop(0, 4, right_t, 0)
        for d in (1, 3, 2):
            yt.append(
                remote(
                    gathered_t.at[2 * y + half],
                    gathered_t.at[2 * y + half],
                    yt_send.at[half, d - 1],
                    yt_recv.at[half, d - 1],
                    at(d, 0, 0, 0),
                )
            )
        stage_two(2 + half)

    for copy in yt:
        copy.wait_recv()
    for p in range(2):

        agg_theta[p] = left(gathered_t, p)

    outs = []
    for half in range(2):
        arrived(2 + half)

        def finish(c, carry, half=half):
            cols = pl.ds(pl.multiple_of(c * 256, 256), 256)
            a = right(2 + half, c)
            scale = jnp.sqrt(var_rows[pl.ds(half * 256, 256), :] * var_cols[:, cols])
            inverse = lax.rsqrt(scale * scale + a * a)
            size = jnp.abs(a)
            angle = arc(jnp.minimum(size, scale) / jnp.maximum(size, scale))
            angle = jnp.where(size > scale, (math.pi / 2) - angle, angle)
            share = 0.5 + jnp.where(a < 0, -angle, angle) * (1 / math.pi)
            kern = scale * (scale * inverse * (1 / math.pi) + share * (a * inverse))
            out_n[half, :, cols] = kern
            out_k[half, :, cols] = kern + agg_theta[half, :, cols] * share
            return carry

        lax.fori_loop(0, 4, finish, 0)
        rows = pl.ds(half * 256, 256)
        outs.append(load(out_n.at[half], nngp.at[rows], out_sem.at[half, 0]))
        outs.append(load(out_k.at[half], ntk.at[rows], out_sem.at[half, 1]))

    for copy in ys + yt:
        copy.wait_send()
    for copy in first.values():
        copy.wait_send()
    for (ph, st, j), copy in second.items():
        if ph >= 2:
            copy.wait_send()
    for copy in outs:
        copy.wait()


def shards(sigma_in, theta_in, var_rows, var_cols, row_nbrs, row_vals, col_nbrs, col_vals):
    rank_col = lax.axis_index("cols")
    entries = col_nbrs.reshape(32, 80)
    owner, within = entries // 4, entries % 4
    want = jnp.max(
        jnp.where(owner[:, None, :] == jnp.arange(32, dtype=jnp.int32)[None, :, None], within[:, None, :], 0), axis=2
    ).reshape(1024)
    mine = lax.dynamic_slice_in_dim(entries, rank_col, 1, 0)[0]
    own, block = mine // 4, mine % 4
    oz, ox, oc = own // 8, (own // 2) % 4, own % 2
    index_a = jnp.where(own == rank_col, 32 + block, (ox * 2 + oc) * 4 + oz)
    index_b = jnp.where(own == rank_col, 32 + block, (oz * 2 + oc) * 4 + ox)
    index = jnp.concatenate([index_a, index_b])

    smem = pl.BlockSpec(memory_space=pltpu.SMEM)
    vmem = pl.BlockSpec(memory_space=pltpu.VMEM)
    hbm = pl.BlockSpec(memory_space=pl.ANY)
    dma = pltpu.SemaphoreType.DMA
    out = jax.ShapeDtypeStruct((512, 1024), F32)
    return pl.pallas_call(
        kernel,
        out_shape=(out, out),
        in_specs=[smem, smem, smem, hbm, hbm, vmem, vmem, hbm, hbm],
        out_specs=(hbm, hbm),
        scratch_shapes=[
            pltpu.VMEM((80, 256, 256), BF16),
            pltpu.VMEM((6, 256, 256), BF16),
            pltpu.VMEM((8, 256, 1024), BF16),
            pltpu.VMEM((8, 256, 1024), BF16),
            pltpu.VMEM((2, 256, 1024), F32),
            pltpu.VMEM((2, 256, 1024), F32),
            pltpu.VMEM((2, 256, 1024), F32),
        ]
        + [pltpu.VMEM((4, 4, 128, 256), BF16)] * 8
        + [pltpu.VMEM((36, 128, 256), BF16)] * 8
        + [pltpu.VMEM((7, 4, 128, 256), BF16)] * 4
        + [
            dma((4,)),
            dma((2,)),
            dma((3, 2, 4)),
            dma((2, 3)),
            dma((2, 3)),
            dma((2, 3)),
            dma((2, 3)),
            dma((4, 2, 3)),
            dma((4, 2, 3)),
            dma((4, 2, 7)),
            dma((4, 2, 7)),
            dma((2, 2)),
        ],
        compiler_params=pltpu.CompilerParams(
            collective_id=0, has_side_effects=True, vmem_limit_bytes=62 * 1024 * 1024
        ),
    )(
        want,
        index,
        row_nbrs.reshape(24),
        theta_in,
        sigma_in,
        var_rows.reshape(512, 1),
        var_cols.reshape(1, 1024),
        row_vals,
        col_vals,
    )


def solution(mesh):
    in_specs = (
        P("rows", "cols"),
        P("rows", "cols"),
        P("rows"),
        P("cols"),
        P(),
        P(),
        P(),
        P("cols", None, None, None),
    )
    out_specs = (P("rows", "cols"), P("rows", "cols"))
    return jax.shard_map(shards, mesh=mesh, in_specs=in_specs, out_specs=out_specs, check_vma=False)
```

```python
import functools
import math

import jax
import jax.numpy as jnp
from jax import lax
from jax.experimental import pallas as pl
from jax.experimental.pallas import tpu as pltpu
from jax.sharding import PartitionSpec as P

MESH = pl.DeviceIdType.MESH
BF16 = jnp.bfloat16
F32 = jnp.float32

ATAN = (
    0.9999998979,
    -0.3333196033,
    0.1996924122,
    -0.1401660921,
    0.09906147193,
    -0.05936764426,
    0.02416647519,
    -0.004668829048,
)


def arc(t):
    t2 = t * t
    total = jnp.full_like(t, ATAN[-1])
    for c in ATAN[-2::-1]:
        total = total * t2 + c
    return total * t


def kernel(
    col_nbrs, row_nbrs, theta, sigma, row_vals, col_vals,
    agg_s, agg_t,
    wanted, weights, row_weights, gathered_s, gathered_t, total_s, total_t,
    pa0, pa1, pa2, pa3, pb0, pb1, pb2, pb3,
    ra0, ra1, ra2, ra3, rb0, rb1, rb2, rb3,
    sa0, sa1, sb0, sb1,
    w_sem, rv_sem, own_sem, ys_send, ys_recv, yt_send, yt_recv,
    one_send, one_recv, two_send, two_recv, out_sem,
):
    pools = ((pa0, pb0), (pa1, pb1), (pa2, pb2), (pa3, pb3))
    slots = ((ra0, rb0), (ra1, rb1), (ra2, rb2), (ra3, rb3))
    sends = ((sa0, sb0), (sa1, sb1), (sa0, sb0), (sa1, sb1))
    y = lax.axis_index("rows")
    col = lax.axis_index("cols")
    z, x, core = col // 8, (col // 2) % 4, col % 2
    mine = (z, x)

    def at(dy, dz, dx, dc):
        return (
            lax.rem(y + dy, 4),
            (lax.rem(z + dz, 4) * 4 + lax.rem(x + dx, 4)) * 2 + lax.rem(core + dc, 2),
        )

    def line(st, d, dc):
        return at(0, d, 0, dc) if st == 0 else at(0, 0, d, dc)

    def local(src, dst, sem):
        copy = pltpu.make_async_copy(src, dst, sem)
        copy.start()
        return copy

    def remote(src, dst, ssem, rsem, device):
        copy = pltpu.make_async_remote_copy(
            src_ref=src, dst_ref=dst, send_sem=ssem, recv_sem=rsem, device_id=device, device_id_type=MESH
        )
        copy.start()
        return copy

    own_pool = [
        local(
            theta.at[pl.ds(ph * 256 + st * 128, 128), pl.ds(b * 256, 256)],
            pools[ph][st].at[mine[st], b],
            own_sem.at[ph, st, b],
        )
        for ph in range(2)
        for st in range(2)
        for b in range(4)
    ]

    barrier = pltpu.get_barrier_semaphore()
    partners = [(dy, 0, 0, 0) for dy in (1, 2, 3)]
    partners += [(0, dz, 0, dc) for dz in (1, 2, 3) for dc in (0, 1)]
    partners += [(0, 0, dx, dc) for dx in (1, 2, 3) for dc in (0, 1)]
    partners += [(0, 0, 0, 1)]
    for p in partners:
        pl.semaphore_signal(barrier, inc=1, device_id=at(*p), device_id_type=MESH)
    pl.semaphore_wait(barrier, len(partners))

    first = {}
    second = {}

    def step(ph, st, way, src, blocks):
        part = pools[ph][st].at[src] if blocks is None else pools[ph][st].at[src, pl.ds(blocks, 2)]
        first[ph, st, way] = remote(
            part, part, one_send.at[ph, st, way], one_recv.at[ph, st, way], line(st, (1, 3)[way % 2], 0)
        )

    def stage_one(ph):
        for st in range(2):
            step(ph, st, 0, mine[st], None)
            step(ph, st, 1, mine[st], None)

    def forward(ph):
        for st in range(2):
            first[ph, st, 0].wait_recv()
            step(ph, st, 2, lax.rem(mine[st] + 3, 4), 0)
        for st in range(2):
            first[ph, st, 1].wait_recv()
            step(ph, st, 3, lax.rem(mine[st] + 1, 4), 2)

    def source_at(st, s):
        return ((s * 4 + x) if st == 0 else (z * 4 + s)) * 2 + core

    def look(st):
        def one(j, carry):
            other = line(1 - st, j // 2, j % 2)[1]
            sources = [source_at(st, s) for s in range(4)]

            def entry(i, found):
                for k in range(20):
                    n = col_nbrs[k, other * 4 + i]
                    owner, block = n // 4, n % 4
                    found = tuple(jnp.where(owner == s, block, f) for s, f in zip(sources, found))
                return found

            found = lax.fori_loop(0, 4, entry, (jnp.int32(0),) * 4)
            for s in range(4):
                wanted[(st * 8 + j) * 4 + s] = found[s]
            return carry

        lax.fori_loop(0, 8, one, 0)

    def stage_two(ph):
        for st in range(2):
            first[ph, st, 2].wait_recv()
            first[ph, st, 3].wait_recv()
            pool, out, here = pools[ph][st], sends[ph][st], slots[ph][st]
            place = mine[1 - st] * 2 + core
            if ph >= 2:
                for j in range(1, 8):
                    second[ph - 2, st, j].wait_send()

            def pack(i, carry):
                j, s = i // 4 + 1, i % 4
                out[j - 1, s] = pool[s, wanted[(st * 8 + j) * 4 + s]]
                return carry

            lax.fori_loop(0, 28, pack, 0)
            for j in (2, 3, 6, 7, 4, 5, 1):
                second[ph, st, j] = remote(
                    out.at[j - 1],
                    here.at[pl.ds(place * 4, 4)],
                    two_send.at[ph, st, j - 1],
                    two_recv.at[ph, st, j - 1],
                    line(1 - st, j // 2, j % 2),
                )
        for st in range(2):
            pool, here = pools[ph][st], slots[ph][st]
            place = mine[1 - st] * 2 + core
            for s in range(4):
                here[place * 4 + s] = pool[s, wanted[st * 32 + s]]
            for b in range(4):
                here[32 + b] = pool[mine[st], b]

    def arrived(ph):
        for st in range(2):
            for j in range(1, 8):
                second[ph, st, j].wait_recv()

    def right(ph, c):
        here_a, here_b = slots[ph]
        total = None
        for k in range(20):
            n = col_nbrs[k, col * 4 + c]
            owner, block = n // 4, n % 4
            oz, ox, oc = owner // 8, (owner // 2) % 4, owner % 2
            index_a = jnp.where(owner == col, 32 + block, (ox * 2 + oc) * 4 + oz)
            index_b = jnp.where(owner == col, 32 + block, (oz * 2 + oc) * 4 + ox)
            lhs = jnp.concatenate([here_a[index_a], here_b[index_b]], axis=0)
            part = lax.dot_general(
                lhs, weights[c * 20 + k], (((1,), (1,)), ((), ())), preferred_element_type=F32
            )
            total = part if total is None else total + part
        return total

    def left(gathered, p):
        total = None
        for k in range(3):
            n = row_nbrs[k, 2 * y + p]
            part = jnp.dot(row_weights[p * 3 + k], gathered[n], preferred_element_type=F32)
            total = part if total is None else total + part
        return total

    for copy in own_pool:
        copy.wait()
    for ph in range(2):
        stage_one(ph)
    ys = [
        remote(
            sigma.at[pl.ds(half * 256, 256)],
            gathered_s.at[2 * y + half],
            ys_send.at[half, d - 1],
            ys_recv.at[half, d - 1],
            at(d, 0, 0, 0),
        )
        for half in range(2)
        for d in (1, 3, 2)
    ]
    loads = [
        local(sigma.at[pl.ds(half * 256, 256)], gathered_s.at[2 * y + half], own_sem.at[2, half, 0])
        for half in range(2)
    ]
    loads += [local(row_vals.at[2 * y + p], row_weights.at[pl.ds(p * 3, 3)], rv_sem.at[p]) for p in range(2)]
    loads += [local(col_vals.at[c], weights.at[pl.ds(c * 20, 20)], w_sem.at[c]) for c in range(4)]

    look(0)
    look(1)
    forward(0)
    forward(1)
    stage_two(0)
    stage_two(1)

    for copy in loads:
        copy.wait()
    for copy in ys:
        copy.wait_recv()
    for p in range(2):
        panel = left(gathered_s, p).astype(BF16)
        for st in range(2):
            for b in range(4):
                pools[2 + p][st][mine[st], b] = panel[st * 128 : (st + 1) * 128, b * 256 : (b + 1) * 256]
        stage_one(2 + p)

    yt = []

    def right_theta(half):
        arrived(half)

        def one(c, carry):
            cols = pl.ds(pl.multiple_of(c * 256, 256), 256)
            gathered_t[2 * y + half, :, cols] = right(half, c).astype(BF16)
            return carry

        lax.fori_loop(0, 4, one, 0)
        for d in (1, 3, 2):
            yt.append(
                remote(
                    gathered_t.at[2 * y + half],
                    gathered_t.at[2 * y + half],
                    yt_send.at[half, d - 1],
                    yt_recv.at[half, d - 1],
                    at(d, 0, 0, 0),
                )
            )

    right_theta(0)
    forward(2)
    forward(3)
    stage_two(2)
    right_theta(1)
    stage_two(3)

    for copy in yt:
        copy.wait_recv()
    outs = []
    for p in range(2):
        total_t[p] = left(gathered_t, p)
        outs.append(local(total_t.at[p], agg_t.at[pl.ds(p * 256, 256)], out_sem.at[p, 0]))

    for half in range(2):
        arrived(2 + half)

        def finish(c, carry, half=half):
            cols = pl.ds(pl.multiple_of(c * 256, 256), 256)
            total_s[half, :, cols] = right(2 + half, c)
            return carry

        lax.fori_loop(0, 4, finish, 0)
        outs.append(local(total_s.at[half], agg_s.at[pl.ds(half * 256, 256)], out_sem.at[half, 1]))

    for copy in ys + yt:
        copy.wait_send()
    for copy in first.values():
        copy.wait_send()
    for (ph, st, j), copy in second.items():
        if ph >= 2:
            copy.wait_send()
    for copy in outs:
        copy.wait()


def update(agg_s, agg_t, var_rows, var_cols, nngp, ntk):
    rows = agg_s.shape[0]
    place = [lax.broadcasted_iota(jnp.int32, (rows, rows), i) for i in range(2)]
    at_rows = jnp.sum(jnp.where(place[0] == place[1], var_rows[...], 0.0), axis=1, keepdims=True)
    a = agg_s[...]
    scale = jnp.sqrt(at_rows * var_cols[...])
    inverse = lax.rsqrt(scale * scale + a * a)
    size = jnp.abs(a)
    angle = arc(jnp.minimum(size, scale) / jnp.maximum(size, scale))
    angle = jnp.where(size > scale, (math.pi / 2) - angle, angle)
    share = 0.5 + jnp.where(a < 0, -angle, angle) * (1 / math.pi)
    kern = scale * (scale * inverse * (1 / math.pi) + share * (a * inverse))
    nngp[...] = kern
    ntk[...] = kern + agg_t[...] * share


def shards(sigma_in, theta_in, var_rows, var_cols, row_nbrs, row_vals, col_nbrs, col_vals):
    smem = pl.BlockSpec(memory_space=pltpu.SMEM)
    hbm = pl.BlockSpec(memory_space=pl.ANY)
    dma = pltpu.SemaphoreType.DMA
    out = jax.ShapeDtypeStruct((512, 1024), F32)
    agg_s, agg_t = pl.pallas_call(
        kernel,
        out_shape=(out, out),
        in_specs=[smem, smem, hbm, hbm, hbm, hbm],
        out_specs=(hbm, hbm),
        scratch_shapes=[
            pltpu.SMEM((64,), jnp.int32),
            pltpu.VMEM((80, 256, 256), BF16),
            pltpu.VMEM((6, 256, 256), BF16),
            pltpu.VMEM((8, 256, 1024), BF16),
            pltpu.VMEM((8, 256, 1024), BF16),
            pltpu.VMEM((2, 256, 1024), F32),
            pltpu.VMEM((2, 256, 1024), F32),
        ]
        + [pltpu.VMEM((4, 4, 128, 256), BF16)] * 8
        + [pltpu.VMEM((36, 128, 256), BF16)] * 8
        + [pltpu.VMEM((7, 4, 128, 256), BF16)] * 4
        + [
            dma((4,)),
            dma((2,)),
            dma((3, 2, 4)),
            dma((2, 3)),
            dma((2, 3)),
            dma((2, 3)),
            dma((2, 3)),
            dma((4, 2, 4)),
            dma((4, 2, 4)),
            dma((4, 2, 7)),
            dma((4, 2, 7)),
            dma((2, 2)),
        ],
        compiler_params=pltpu.CompilerParams(
            collective_id=0, has_side_effects=True, vmem_limit_bytes=62 * 1024 * 1024
        ),
    )(col_nbrs.T, row_nbrs.T, theta_in, sigma_in, row_vals, col_vals)

    rows = 128
    block = pl.BlockSpec((rows, 1024), lambda i: (i, 0))
    return pl.pallas_call(
        update,
        grid=(512 // rows,),
        out_shape=(out, out),
        in_specs=[
            block,
            block,
            pl.BlockSpec((1, rows), lambda i: (0, i)),
            pl.BlockSpec((1, 1024), lambda i: (0, 0)),
        ],
        out_specs=(block, block),
        compiler_params=pltpu.CompilerParams(vmem_limit_bytes=62 * 1024 * 1024),
    )(agg_s, agg_t, var_rows.reshape(1, 512), var_cols.reshape(1, 1024))


def solution(mesh):
    in_specs = (
        P("rows", "cols"),
        P("rows", "cols"),
        P("rows"),
        P("cols"),
        P(),
        P(),
        P(),
        P("cols", None, None, None),
    )
    out_specs = (P("rows", "cols"), P("rows", "cols"))
    return jax.shard_map(shards, mesh=mesh, in_specs=in_specs, out_specs=out_specs, check_vma=False)
```

```python
import functools
import math

import jax
import jax.numpy as jnp
from jax import lax
from jax.experimental import pallas as pl
from jax.experimental.pallas import tpu as pltpu
from jax.sharding import PartitionSpec as P

MESH = pl.DeviceIdType.MESH
BF16 = jnp.bfloat16
F32 = jnp.float32

ATAN = (
    0.9999998979,
    -0.3333196033,
    0.1996924122,
    -0.1401660921,
    0.09906147193,
    -0.05936764426,
    0.02416647519,
    -0.004668829048,
)


INNER = ((0, 0), (0, 1), (0, 3), (1, 1), (3, 3), (2, 1))
HOPS = ((0, (0, 1)), (0, (0, 3)), (1, (1, 0)), (2, (3, 0)), (3, (1, 0)))
OUTER = (((1, 0), (2,)), ((3, 0), (4, 0, 1)), ((0, 1), (1, 3, 5)), ((0, 3), (3, 5, 4)))
PARTS = []
for way, places in OUTER:
    for flip in (0, 1):
        PARTS.append((way, flip, places, sum(len(p[2]) for p in PARTS)))
PARTS.append(((0, 0), 1, (0, 1, 2, 3, 4, 5), 20))
PARTS.append(((0, 0), 0, (1, 2, 3, 4, 5), 26))
OWN = 31
SLOTS = 35


def slot_table():
    table = {}
    for way, flip, places, start in PARTS:
        for i, p in enumerate(places):
            offset = tuple((a + b) % 4 for a, b in zip(INNER[p], way))
            table[offset, flip] = start + i
    table[(0, 0), 0] = OWN
    return table


def arc(t):
    t2 = t * t
    total = jnp.full_like(t, ATAN[-1])
    for c in ATAN[-2::-1]:
        total = total * t2 + c
    return total * t


def kernel(
    col_nbrs, row_nbrs, theta, sigma, row_vals, col_vals,
    agg_s, agg_t,
    wanted, table, weights, row_weights, gathered_s, gathered_t, total,
    pa0, pa1, pa2, pa3, pb0, pb1, pb2, pb3,
    fa0, fa1, fa2, fa3, fb0, fb1, fb2, fb3,
    ra0, ra1, ra2, ra3, rb0, rb1, rb2, rb3,
    sa0, sa1, sb0, sb1,
    w_sem, rv_sem, own_sem, ys_send, ys_recv, yt_send, yt_recv,
    one_send, one_recv, two_send, two_recv, out_sem,
):
    pools = ((pa0, pb0), (pa1, pb1), (pa2, pb2), (pa3, pb3))
    fars = ((fa0, fb0), (fa1, fb1), (fa2, fb2), (fa3, fb3))
    slots = ((ra0, rb0), (ra1, rb1), (ra2, rb2), (ra3, rb3))
    sends = ((sa0, sb0), (sa1, sb1), (sa0, sb0), (sa1, sb1))
    y = lax.axis_index("rows")
    col = lax.axis_index("cols")
    z, x, core = col // 8, (col // 2) % 4, col % 2

    def at(dy, dz, dx, dc):
        return (
            lax.rem(y + dy, 4),
            (lax.rem(z + dz, 4) * 4 + lax.rem(x + dx, 4)) * 2 + lax.rem(core + dc, 2),
        )

    def toward(st, way, flip):
        return at(0, way[st], way[1 - st], flip)

    def local(src, dst, sem):
        copy = pltpu.make_async_copy(src, dst, sem)
        copy.start()
        return copy

    def remote(src, dst, ssem, rsem, device):
        copy = pltpu.make_async_remote_copy(
            src_ref=src, dst_ref=dst, send_sem=ssem, recv_sem=rsem, device_id=device, device_id_type=MESH
        )
        copy.start()
        return copy

    own_pool = [
        local(
            theta.at[pl.ds(ph * 256 + st * 128, 128), pl.ds(b * 256, 256)],
            pools[ph][st].at[0, b],
            own_sem.at[ph, st, b],
        )
        for ph in range(2)
        for st in range(2)
        for b in range(4)
    ]

    barrier = pltpu.get_barrier_semaphore()
    partners = [(dy, 0, 0, 0) for dy in (1, 2, 3)] + [(0, 0, 0, 1)]
    partners += [(0, d, 0, dc) for d in (1, 3) for dc in (0, 1)]
    partners += [(0, 0, d, dc) for d in (1, 3) for dc in (0, 1)]
    for p in partners:
        pl.semaphore_signal(barrier, inc=1, device_id=at(*p), device_id_type=MESH)
    pl.semaphore_wait(barrier, len(partners))

    first = {}
    second = {}

    def held(ph, st, place):
        return fars[ph][st] if place == 5 else pools[ph][st].at[place]

    def chosen(ph, st, place, block):
        return fars[ph][st][block] if place == 5 else pools[ph][st][place, block]

    def hop(ph, i):
        for st in range(2):
            src, way = HOPS[i]
            if src:
                first[ph, st, src - 1].wait_recv()
            first[ph, st, i] = remote(
                held(ph, st, src), held(ph, st, i + 1), one_send.at[ph, st, i], one_recv.at[ph, st, i], toward(st, way, 0)
            )

    def hop_one(ph):
        hop(ph, 0)
        hop(ph, 1)

    def hop_two(ph):
        hop(ph, 2)
        hop(ph, 3)

    def look(parts):
        for m in parts:
            for st in range(2):
                way, flip, places, start = PARTS[m]
                other = toward(st, way, flip)[1]
                sources = [toward(st, tuple((4 - o) % 4 for o in INNER[place]), 0)[1] for place in places]

                def entry(i, found, other=other, sources=sources):
                    for k in range(20):
                        n = col_nbrs[k, other * 4 + i]
                        owner, block = n // 4, n % 4
                        found = tuple(jnp.where(owner == s, block, f) for s, f in zip(sources, found))
                    return found

                found = lax.fori_loop(0, 4, entry, (jnp.int32(0),) * len(places))
                for i, f in enumerate(found):
                    wanted[st * 32 + start + i] = f

    def serve(ph, parts):
        for st in range(2):
            out, here = sends[ph][st], slots[ph][st]
            for m in parts:
                way, flip, places, start = PARTS[m]
                if ph >= 2:
                    second[ph - 2, st, m].wait_send()
                for i, place in enumerate(places):
                    out[start + i] = chosen(ph, st, place, wanted[st * 32 + start + i])
                part = pl.ds(start, len(places))
                second[ph, st, m] = remote(
                    out.at[part], here.at[part], two_send.at[ph, st, m], two_recv.at[ph, st, m], toward(st, way, flip)
                )

    def serve_one(ph):
        for st in range(2):
            first[ph, st, 3].wait_recv()
        serve(ph, (2, 3, 0, 1))

    def serve_two(ph):
        for st in range(2):
            first[ph, st, 4].wait_recv()
        serve(ph, (4, 6, 5, 7, 8))
        for st in range(2):
            here = slots[ph][st]
            for i, place in enumerate(PARTS[9][2]):
                here[PARTS[9][3] + i] = chosen(ph, st, place, wanted[st * 32 + PARTS[9][3] + i])
            for b in range(4):
                here[OWN + b] = pools[ph][st][0, b]

    def arrived(ph):
        for st in range(2):
            for m in range(9):
                second[ph, st, m].wait_recv()

    def right(ph, c):
        here_a, here_b = slots[ph]
        total = None
        for k in range(20):
            n = col_nbrs[k, col * 4 + c]
            owner, block = n // 4, n % 4
            extra = jnp.where(owner == col, block, 0)
            index_a = table[owner] + extra
            index_b = table[32 + owner] + extra
            lhs = jnp.concatenate([here_a[index_a], here_b[index_b]], axis=0)
            part = lax.dot_general(
                lhs, weights[c * 20 + k], (((1,), (1,)), ((), ())), preferred_element_type=F32
            )
            total = part if total is None else total + part
        return total

    def left(gathered, p):
        total = None
        for k in range(3):
            n = row_nbrs[k, 2 * y + p]
            part = jnp.dot(row_weights[p * 3 + k], gathered[n], preferred_element_type=F32)
            total = part if total is None else total + part
        return total

    for copy in own_pool:
        copy.wait()
    hop_one(0)
    hop_one(1)
    ys = [
        remote(
            sigma.at[pl.ds(half * 256, 256)],
            gathered_s.at[2 * y + half],
            ys_send.at[half, d - 1],
            ys_recv.at[half, d - 1],
            at(d, 0, 0, 0),
        )
        for half in range(2)
        for d in (1, 3, 2)
    ]
    loads = [
        local(sigma.at[pl.ds(half * 256, 256)], gathered_s.at[2 * y + half], own_sem.at[2, half, 0])
        for half in range(2)
    ]
    loads += [local(row_vals.at[2 * y + p], row_weights.at[pl.ds(p * 3, 3)], rv_sem.at[p]) for p in range(2)]
    loads += [local(col_vals.at[c], weights.at[pl.ds(c * 20, 20)], w_sem.at[c]) for c in range(4)]

    look((0, 1, 2, 3))
    hop_two(0)
    look((4, 5, 6, 7))
    hop_two(1)
    hop(0, 4)
    serve_one(0)
    hop(1, 4)
    serve_one(1)
    look((8, 9))
    serve_two(0)
    serve_two(1)

    slot_of = slot_table()
    for dz in range(4):
        for dx in range(4):
            for flip in range(2):
                owner = at(0, (4 - dz) % 4, (4 - dx) % 4, flip)[1]
                table[owner] = slot_of[(dz, dx), flip]
                table[32 + owner] = slot_of[(dx, dz), flip]

    for copy in loads:
        copy.wait()
    for copy in ys:
        copy.wait_recv()
    for p in range(2):
        panel = left(gathered_s, p).astype(BF16)
        for st in range(2):
            for b in range(4):
                pools[2 + p][st][0, b] = panel[st * 128 : (st + 1) * 128, b * 256 : (b + 1) * 256]
        hop_one(2 + p)

    yt = []

    def right_theta(half):
        arrived(half)

        def one(c, carry):
            cols = pl.ds(pl.multiple_of(c * 256, 256), 256)
            gathered_t[2 * y + half, :, cols] = right(half, c).astype(BF16)
            return carry

        lax.fori_loop(0, 4, one, 0)
        for d in (1, 3, 2):
            yt.append(
                remote(
                    gathered_t.at[2 * y + half],
                    gathered_t.at[2 * y + half],
                    yt_send.at[half, d - 1],
                    yt_recv.at[half, d - 1],
                    at(d, 0, 0, 0),
                )
            )

    right_theta(0)
    hop_two(2)
    hop_two(3)
    hop(2, 4)
    serve_one(2)
    hop(3, 4)
    serve_one(3)
    serve_two(2)
    right_theta(1)
    serve_two(3)

    for copy in yt:
        copy.wait_recv()
    outs = []
    for p in range(2):
        total[p] = left(gathered_t, p)
        outs.append(local(total.at[p], agg_t.at[pl.ds(p * 256, 256)], out_sem.at[p, 0]))

    for half in range(2):
        arrived(2 + half)
        outs[half].wait()

        def finish(c, carry, half=half):
            cols = pl.ds(pl.multiple_of(c * 256, 256), 256)
            total[half, :, cols] = right(2 + half, c)
            return carry

        lax.fori_loop(0, 4, finish, 0)
        outs.append(local(total.at[half], agg_s.at[pl.ds(half * 256, 256)], out_sem.at[half, 1]))

    for copy in ys + yt:
        copy.wait_send()
    for copy in first.values():
        copy.wait_send()
    for (ph, st, j), copy in second.items():
        if ph >= 2:
            copy.wait_send()
    for copy in outs[2:]:
        copy.wait()


def update(agg_s, agg_t, var_rows, var_cols, nngp, ntk, s_in, t_in, n_out, k_out, in_sem, out_sem):
    rows = 64
    parts = 512 // rows
    loads = []
    for i in range(parts):
        for j, (src, dst) in enumerate(((agg_s, s_in), (agg_t, t_in))):
            copy = pltpu.make_async_copy(src.at[pl.ds(i * rows, rows)], dst.at[i], in_sem.at[i, j])
            copy.start()
            loads.append(copy)
    place = [lax.broadcasted_iota(jnp.int32, (128, 128), i) for i in range(2)]
    scale_cols = jnp.sqrt(var_cols[...])
    stores = []
    for i in range(parts):
        at, lane = i * rows % 128, i * rows // 128 * 128
        spread = jnp.where(place[0] == place[1], var_rows[:, lane : lane + 128], 0.0)[at : at + rows]
        scale = jnp.sqrt(jnp.sum(spread, axis=1, keepdims=True)) * scale_cols
        loads[2 * i].wait()
        loads[2 * i + 1].wait()
        a = s_in[i]
        square = scale * scale + a * a
        inverse = lax.rsqrt(square)
        angle = arc(a / (scale + square * inverse))
        share = 0.5 + angle * (2 / math.pi)
        kern = scale * (scale * inverse * (1 / math.pi) + share * (a * inverse))
        n_out[i] = kern
        k_out[i] = kern + t_in[i] * share
        for j, (src, dst) in enumerate(((n_out, nngp), (k_out, ntk))):
            copy = pltpu.make_async_copy(src.at[i], dst.at[pl.ds(i * rows, rows)], out_sem.at[i, j])
            copy.start()
            stores.append(copy)
    for copy in stores:
        copy.wait()


def shards(sigma_in, theta_in, var_rows, var_cols, row_nbrs, row_vals, col_nbrs, col_vals):
    smem = pl.BlockSpec(memory_space=pltpu.SMEM)
    hbm = pl.BlockSpec(memory_space=pl.ANY)
    dma = pltpu.SemaphoreType.DMA
    out = jax.ShapeDtypeStruct((512, 1024), F32)
    agg_s, agg_t = pl.pallas_call(
        kernel,
        out_shape=(out, out),
        in_specs=[smem, smem, hbm, hbm, hbm, hbm],
        out_specs=(hbm, hbm),
        scratch_shapes=[
            pltpu.SMEM((64,), jnp.int32),
            pltpu.SMEM((64,), jnp.int32),
            pltpu.VMEM((80, 256, 256), BF16),
            pltpu.VMEM((6, 256, 256), BF16),
            pltpu.VMEM((8, 256, 1024), BF16),
            pltpu.VMEM((8, 256, 1024), BF16),
            pltpu.VMEM((2, 256, 1024), F32),
        ]
        + [pltpu.VMEM((5, 4, 128, 256), BF16)] * 8
        + [pltpu.VMEM((4, 128, 256), BF16)] * 8
        + [pltpu.VMEM((SLOTS, 128, 256), BF16)] * 8
        + [pltpu.VMEM((26, 128, 256), BF16)] * 4
        + [
            dma((4,)),
            dma((2,)),
            dma((3, 2, 4)),
            dma((2, 3)),
            dma((2, 3)),
            dma((2, 3)),
            dma((2, 3)),
            dma((4, 2, 5)),
            dma((4, 2, 5)),
            dma((4, 2, 9)),
            dma((4, 2, 9)),
            dma((2, 2)),
        ],
        compiler_params=pltpu.CompilerParams(
            collective_id=0, has_side_effects=True, vmem_limit_bytes=62 * 1024 * 1024
        ),
    )(col_nbrs.T, row_nbrs.T, theta_in, sigma_in, row_vals, col_vals)

    vmem = pl.BlockSpec(memory_space=pltpu.VMEM)
    return pl.pallas_call(
        update,
        out_shape=(out, out),
        in_specs=[hbm, hbm, vmem, vmem],
        out_specs=(hbm, hbm),
        scratch_shapes=[pltpu.VMEM((8, 64, 1024), F32)] * 4 + [dma((8, 2)), dma((8, 2))],
        compiler_params=pltpu.CompilerParams(vmem_limit_bytes=62 * 1024 * 1024),
    )(agg_s, agg_t, var_rows.reshape(1, 512), var_cols.reshape(1, 1024))


def solution(mesh):
    in_specs = (
        P("rows", "cols"),
        P("rows", "cols"),
        P("rows"),
        P("cols"),
        P(),
        P(),
        P(),
        P("cols", None, None, None),
    )
    out_specs = (P("rows", "cols"), P("rows", "cols"))
    return jax.shard_map(shards, mesh=mesh, in_specs=in_specs, out_specs=out_specs, check_vma=False)
```

```python
import functools
import math

import jax
import jax.numpy as jnp
from jax import lax
from jax.experimental import pallas as pl
from jax.experimental.pallas import tpu as pltpu
from jax.sharding import PartitionSpec as P

MESH = pl.DeviceIdType.MESH
BF16 = jnp.bfloat16
F32 = jnp.float32

ATAN = (
    0.9999998979,
    -0.3333196033,
    0.1996924122,
    -0.1401660921,
    0.09906147193,
    -0.05936764426,
    0.02416647519,
    -0.004668829048,
)


INNER = ((0, 0), (0, 1), (0, 3), (1, 1), (3, 3), (2, 1))
HOPS = ((0, (0, 1)), (0, (0, 3)), (1, (1, 0)), (2, (3, 0)), (3, (1, 0)))
OUTER = (((1, 0), (2,)), ((3, 0), (4, 0, 1)), ((0, 1), (1, 3, 5)), ((0, 3), (3, 5, 4)))
PARTS = []
for way, places in OUTER:
    for flip in (0, 1):
        PARTS.append((way, flip, places, sum(len(p[2]) for p in PARTS)))
PARTS.append(((0, 0), 1, (0, 1, 2, 3, 4, 5), 20))
PARTS.append(((0, 0), 0, (1, 2, 3, 4, 5), 26))
OWN = 31
SLOTS = 35


def slot_table():
    table = {}
    for way, flip, places, start in PARTS:
        for i, p in enumerate(places):
            offset = tuple((a + b) % 4 for a, b in zip(INNER[p], way))
            table[offset, flip] = start + i
    table[(0, 0), 0] = OWN
    return table


def arc(t):
    t2 = t * t
    total = jnp.full_like(t, ATAN[-1])
    for c in ATAN[-2::-1]:
        total = total * t2 + c
    return total * t


def kernel(
    col_nbrs, row_nbrs, theta, sigma, row_vals, col_vals,
    agg_s, agg_t,
    wanted, table, weights, row_weights, gathered_s, gathered_t, total_s, total_t,
    pa0, pa1, pa2, pa3, pb0, pb1, pb2, pb3,
    fa0, fa1, fa2, fa3, fb0, fb1, fb2, fb3,
    ra0, ra1, ra2, ra3, rb0, rb1, rb2, rb3,
    sa0, sa1, sb0, sb1,
    w_sem, rv_sem, own_sem, ys_send, ys_recv, yt_send, yt_recv,
    one_send, one_recv, two_send, two_recv, out_sem,
):
    pools = ((pa0, pb0), (pa1, pb1), (pa2, pb2), (pa3, pb3))
    fars = ((fa0, fb0), (fa1, fb1), (fa2, fb2), (fa3, fb3))
    slots = ((ra0, rb0), (ra1, rb1), (ra2, rb2), (ra3, rb3))
    sends = ((sa0, sb0), (sa1, sb1), (sa0, sb0), (sa1, sb1))
    y = lax.axis_index("rows")
    col = lax.axis_index("cols")
    z, x, core = col // 8, (col // 2) % 4, col % 2

    def at(dy, dz, dx, dc):
        return (
            lax.rem(y + dy, 4),
            (lax.rem(z + dz, 4) * 4 + lax.rem(x + dx, 4)) * 2 + lax.rem(core + dc, 2),
        )

    def toward(st, way, flip):
        return at(0, way[st], way[1 - st], flip)

    def local(src, dst, sem):
        copy = pltpu.make_async_copy(src, dst, sem)
        copy.start()
        return copy

    def remote(src, dst, ssem, rsem, device):
        copy = pltpu.make_async_remote_copy(
            src_ref=src, dst_ref=dst, send_sem=ssem, recv_sem=rsem, device_id=device, device_id_type=MESH
        )
        copy.start()
        return copy

    own_pool = [
        local(
            theta.at[pl.ds(ph * 256 + st * 128, 128), pl.ds(b * 256, 256)],
            pools[ph][st].at[0, b],
            own_sem.at[ph, st, b],
        )
        for ph in range(2)
        for st in range(2)
        for b in range(4)
    ]

    barrier = pltpu.get_barrier_semaphore()
    partners = [(dy, 0, 0, 0) for dy in (1, 2, 3)] + [(0, 0, 0, 1)]
    partners += [(0, d, 0, dc) for d in (1, 3) for dc in (0, 1)]
    partners += [(0, 0, d, dc) for d in (1, 3) for dc in (0, 1)]
    for p in partners:
        pl.semaphore_signal(barrier, inc=1, device_id=at(*p), device_id_type=MESH)
    pl.semaphore_wait(barrier, len(partners))

    first = {}
    second = {}

    def held(ph, st, place):
        return fars[ph][st] if place == 5 else pools[ph][st].at[place]

    def chosen(ph, st, place, block):
        return fars[ph][st][block] if place == 5 else pools[ph][st][place, block]

    def hop(ph, i):
        for st in range(2):
            src, way = HOPS[i]
            if src:
                first[ph, st, src - 1].wait_recv()
            first[ph, st, i] = remote(
                held(ph, st, src), held(ph, st, i + 1), one_send.at[ph, st, i], one_recv.at[ph, st, i], toward(st, way, 0)
            )

    def hop_one(ph):
        hop(ph, 0)
        hop(ph, 1)

    def hop_two(ph):
        hop(ph, 2)
        hop(ph, 3)

    def look(parts):
        for m in parts:
            for st in range(2):
                way, flip, places, start = PARTS[m]
                other = toward(st, way, flip)[1]
                sources = [toward(st, tuple((4 - o) % 4 for o in INNER[place]), 0)[1] for place in places]

                def entry(i, found, other=other, sources=sources):
                    for k in range(20):
                        n = col_nbrs[k, other * 4 + i]
                        owner, block = n // 4, n % 4
                        found = tuple(jnp.where(owner == s, block, f) for s, f in zip(sources, found))
                    return found

                found = lax.fori_loop(0, 4, entry, (jnp.int32(0),) * len(places))
                for i, f in enumerate(found):
                    wanted[st * 32 + start + i] = f

    def serve(ph, parts):
        for st in range(2):
            out, here = sends[ph][st], slots[ph][st]
            for m in parts:
                way, flip, places, start = PARTS[m]
                if ph >= 2:
                    second[ph - 2, st, m].wait_send()
                for i, place in enumerate(places):
                    out[start + i] = chosen(ph, st, place, wanted[st * 32 + start + i])
                part = pl.ds(start, len(places))
                second[ph, st, m] = remote(
                    out.at[part], here.at[part], two_send.at[ph, st, m], two_recv.at[ph, st, m], toward(st, way, flip)
                )

    def serve_one(ph):
        for st in range(2):
            first[ph, st, 3].wait_recv()
        serve(ph, (2, 3, 0, 1))

    def serve_two(ph):
        for st in range(2):
            first[ph, st, 4].wait_recv()
        serve(ph, (4, 6, 5, 7, 8))
        for st in range(2):
            here = slots[ph][st]
            for i, place in enumerate(PARTS[9][2]):
                here[PARTS[9][3] + i] = chosen(ph, st, place, wanted[st * 32 + PARTS[9][3] + i])
            for b in range(4):
                here[OWN + b] = pools[ph][st][0, b]

    def arrived(ph):
        for st in range(2):
            for m in range(9):
                second[ph, st, m].wait_recv()

    def right(ph, c):
        here_a, here_b = slots[ph]
        total = None
        for k in range(20):
            n = col_nbrs[k, col * 4 + c]
            owner, block = n // 4, n % 4
            extra = jnp.where(owner == col, block, 0)
            index_a = table[owner] + extra
            index_b = table[32 + owner] + extra
            lhs = jnp.concatenate([here_a[index_a], here_b[index_b]], axis=0)
            part = lax.dot_general(
                lhs, weights[c * 20 + k], (((1,), (1,)), ((), ())), preferred_element_type=F32
            )
            total = part if total is None else total + part
        return total

    def left(gathered, p):
        total = None
        for k in range(3):
            n = row_nbrs[k, 2 * y + p]
            part = jnp.dot(row_weights[p * 3 + k], gathered[n], preferred_element_type=F32)
            total = part if total is None else total + part
        return total

    for copy in own_pool:
        copy.wait()
    hop_one(0)
    hop_one(1)
    ys = [
        remote(
            sigma.at[pl.ds(half * 256, 256)],
            gathered_s.at[2 * y + half],
            ys_send.at[half, d - 1],
            ys_recv.at[half, d - 1],
            at(d, 0, 0, 0),
        )
        for half in range(2)
        for d in (1, 3, 2)
    ]
    loads = [
        local(sigma.at[pl.ds(half * 256, 256)], gathered_s.at[2 * y + half], own_sem.at[2, half, 0])
        for half in range(2)
    ]
    loads += [local(row_vals.at[2 * y + p], row_weights.at[pl.ds(p * 3, 3)], rv_sem.at[p]) for p in range(2)]
    loads += [local(col_vals.at[c], weights.at[pl.ds(c * 20, 20)], w_sem.at[c]) for c in range(4)]

    look((0, 1, 2, 3))
    hop_two(0)
    look((4, 5, 6, 7))
    hop_two(1)
    hop(0, 4)
    serve_one(0)
    look((8, 9))
    serve_two(0)
    hop(1, 4)
    serve_one(1)
    serve_two(1)

    slot_of = slot_table()
    for dz in range(4):
        for dx in range(4):
            for flip in range(2):
                owner = at(0, (4 - dz) % 4, (4 - dx) % 4, flip)[1]
                table[owner] = slot_of[(dz, dx), flip]
                table[32 + owner] = slot_of[(dx, dz), flip]

    for copy in loads:
        copy.wait()
    for copy in ys:
        copy.wait_recv()
    for p in range(2):
        panel = left(gathered_s, p).astype(BF16)
        for st in range(2):
            for b in range(4):
                pools[2 + p][st][0, b] = panel[st * 128 : (st + 1) * 128, b * 256 : (b + 1) * 256]
        hop_one(2 + p)

    yt = []

    def right_theta(half):
        arrived(half)

        def one(c, carry):
            cols = pl.ds(pl.multiple_of(c * 256, 256), 256)
            gathered_t[2 * y + half, :, cols] = right(half, c).astype(BF16)
            return carry

        lax.fori_loop(0, 4, one, 0)
        for d in (1, 3, 2):
            yt.append(
                remote(
                    gathered_t.at[2 * y + half],
                    gathered_t.at[2 * y + half],
                    yt_send.at[half, d - 1],
                    yt_recv.at[half, d - 1],
                    at(d, 0, 0, 0),
                )
            )

    right_theta(0)
    hop_two(2)
    hop_two(3)
    right_theta(1)
    hop(2, 4)
    serve_one(2)
    serve_two(2)
    hop(3, 4)
    serve_one(3)
    serve_two(3)

    outs = []

    def right_sigma(half):
        arrived(2 + half)

        def one(c, carry):
            cols = pl.ds(pl.multiple_of(c * 256, 256), 256)
            total_s[half, :, cols] = right(2 + half, c)
            return carry

        lax.fori_loop(0, 4, one, 0)
        outs.append(local(total_s.at[half], agg_s.at[pl.ds(half * 256, 256)], out_sem.at[half, 1]))

    right_sigma(0)
    for copy in yt:
        copy.wait_recv()
    for p in range(2):
        total_t[p] = left(gathered_t, p)
        outs.append(local(total_t.at[p], agg_t.at[pl.ds(p * 256, 256)], out_sem.at[p, 0]))
    right_sigma(1)

    for copy in ys + yt:
        copy.wait_send()
    for copy in first.values():
        copy.wait_send()
    for (ph, st, j), copy in second.items():
        if ph >= 2:
            copy.wait_send()
    for copy in outs:
        copy.wait()


def update(agg_s, agg_t, var_rows, var_cols, nngp, ntk, s_in, t_in, n_out, k_out, in_sem, out_sem):
    rows = 64
    parts = 512 // rows
    loads = []
    for i in range(parts):
        for j, (src, dst) in enumerate(((agg_s, s_in), (agg_t, t_in))):
            copy = pltpu.make_async_copy(src.at[pl.ds(i * rows, rows)], dst.at[i], in_sem.at[i, j])
            copy.start()
            loads.append(copy)
    place = [lax.broadcasted_iota(jnp.int32, (128, 128), i) for i in range(2)]
    scale_cols = jnp.sqrt(var_cols[...])
    stores = []
    for i in range(parts):
        at, lane = i * rows % 128, i * rows // 128 * 128
        spread = jnp.where(place[0] == place[1], var_rows[:, lane : lane + 128], 0.0)[at : at + rows]
        scale = jnp.sqrt(jnp.sum(spread, axis=1, keepdims=True)) * scale_cols
        loads[2 * i].wait()
        loads[2 * i + 1].wait()
        a = s_in[i]
        square = scale * scale + a * a
        inverse = lax.rsqrt(square)
        angle = arc(a / (scale + square * inverse))
        share = 0.5 + angle * (2 / math.pi)
        kern = scale * (scale * inverse * (1 / math.pi) + share * (a * inverse))
        n_out[i] = kern
        k_out[i] = kern + t_in[i] * share
        for j, (src, dst) in enumerate(((n_out, nngp), (k_out, ntk))):
            copy = pltpu.make_async_copy(src.at[i], dst.at[pl.ds(i * rows, rows)], out_sem.at[i, j])
            copy.start()
            stores.append(copy)
    for copy in stores:
        copy.wait()


def shards(sigma_in, theta_in, var_rows, var_cols, row_nbrs, row_vals, col_nbrs, col_vals):
    smem = pl.BlockSpec(memory_space=pltpu.SMEM)
    hbm = pl.BlockSpec(memory_space=pl.ANY)
    dma = pltpu.SemaphoreType.DMA
    out = jax.ShapeDtypeStruct((512, 1024), F32)
    agg_s, agg_t = pl.pallas_call(
        kernel,
        out_shape=(out, out),
        in_specs=[smem, smem, hbm, hbm, hbm, hbm],
        out_specs=(hbm, hbm),
        scratch_shapes=[
            pltpu.SMEM((64,), jnp.int32),
            pltpu.SMEM((64,), jnp.int32),
            pltpu.VMEM((80, 256, 256), BF16),
            pltpu.VMEM((6, 256, 256), BF16),
            pltpu.VMEM((8, 256, 1024), BF16),
            pltpu.VMEM((8, 256, 1024), BF16),
            pltpu.VMEM((2, 256, 1024), F32),
            pltpu.VMEM((2, 256, 1024), F32),
        ]
        + [pltpu.VMEM((5, 4, 128, 256), BF16)] * 8
        + [pltpu.VMEM((4, 128, 256), BF16)] * 8
        + [pltpu.VMEM((SLOTS, 128, 256), BF16)] * 8
        + [pltpu.VMEM((26, 128, 256), BF16)] * 4
        + [
            dma((4,)),
            dma((2,)),
            dma((3, 2, 4)),
            dma((2, 3)),
            dma((2, 3)),
            dma((2, 3)),
            dma((2, 3)),
            dma((4, 2, 5)),
            dma((4, 2, 5)),
            dma((4, 2, 9)),
            dma((4, 2, 9)),
            dma((2, 2)),
        ],
        compiler_params=pltpu.CompilerParams(
            collective_id=0, has_side_effects=True, vmem_limit_bytes=62 * 1024 * 1024
        ),
    )(col_nbrs.T, row_nbrs.T, theta_in, sigma_in, row_vals, col_vals)

    vmem = pl.BlockSpec(memory_space=pltpu.VMEM)
    return pl.pallas_call(
        update,
        out_shape=(out, out),
        in_specs=[hbm, hbm, vmem, vmem],
        out_specs=(hbm, hbm),
        scratch_shapes=[pltpu.VMEM((8, 64, 1024), F32)] * 4 + [dma((8, 2)), dma((8, 2))],
        compiler_params=pltpu.CompilerParams(vmem_limit_bytes=62 * 1024 * 1024),
    )(agg_s, agg_t, var_rows.reshape(1, 512), var_cols.reshape(1, 1024))


def solution(mesh):
    in_specs = (
        P("rows", "cols"),
        P("rows", "cols"),
        P("rows"),
        P("cols"),
        P(),
        P(),
        P(),
        P("cols", None, None, None),
    )
    out_specs = (P("rows", "cols"), P("rows", "cols"))
    return jax.shard_map(shards, mesh=mesh, in_specs=in_specs, out_specs=out_specs, check_vma=False)
```

```python
import functools
import math

import jax
import jax.numpy as jnp
from jax import lax
from jax.experimental import pallas as pl
from jax.experimental.pallas import tpu as pltpu
from jax.sharding import PartitionSpec as P

MESH = pl.DeviceIdType.MESH
BF16 = jnp.bfloat16
F32 = jnp.float32

ATAN = (
    0.9999998979,
    -0.3333196033,
    0.1996924122,
    -0.1401660921,
    0.09906147193,
    -0.05936764426,
    0.02416647519,
    -0.004668829048,
)


INNER = ((0, 0), (0, 1), (0, 3), (1, 1), (3, 3), (2, 1))
HOPS = ((0, (0, 1)), (0, (0, 3)), (1, (1, 0)), (2, (3, 0)), (3, (1, 0)))
OUTER = (((1, 0), (2,)), ((3, 0), (4, 0, 1)), ((0, 1), (1, 3)), ((0, 3), (3, 4)), ((0, 1), (5,)), ((0, 3), (5,)))
PARTS = []
for way, places in OUTER:
    for flip in (0, 1):
        PARTS.append((way, flip, places, sum(len(p[2]) for p in PARTS)))
PARTS.append(((0, 0), 1, (0, 1, 2, 3, 4, 5), 20))
PARTS.append(((0, 0), 0, (1, 2, 3, 4, 5), 26))
SIBLING, SELF = 12, 13
OWN = 31
SLOTS = 35


def slot_table():
    table = {}
    for way, flip, places, start in PARTS:
        for i, p in enumerate(places):
            offset = tuple((a + b) % 4 for a, b in zip(INNER[p], way))
            table[offset, flip] = start + i
    table[(0, 0), 0] = OWN
    return table


def arc(t):
    t2 = t * t
    total = jnp.full_like(t, ATAN[-1])
    for c in ATAN[-2::-1]:
        total = total * t2 + c
    return total * t


def column(row):
    place = [lax.broadcasted_iota(jnp.int32, (128, 128), i) for i in range(2)]
    return jnp.sum(jnp.where(place[0] == place[1], row, 0.0), axis=1, keepdims=True)


def both(a, t, scale):
    square = scale * scale + a * a
    inverse = lax.rsqrt(square)
    angle = arc(a / (scale + square * inverse))
    share = 0.5 + angle * (2 / math.pi)
    kern = scale * (scale * inverse * (1 / math.pi) + share * (a * inverse))
    return kern, kern + t * share


def kernel(
    col_nbrs, row_nbrs, var_rows, var_cols, theta, sigma, row_vals, col_vals,
    part_s, part_t,
    wanted, table, index, weights, row_weights, gathered_s, gathered_t, total_s, total_t,
    pa0, pa1, pa2, pa3, pb0, pb1, pb2, pb3,
    fa0, fa1, fa2, fa3, fb0, fb1, fb2, fb3,
    ra0, ra1, ra2, ra3, rb0, rb1, rb2, rb3,
    sa0, sa1, sb0, sb1,
    w_sem, rv_sem, own_sem, ys_send, ys_recv, yt_send, yt_recv,
    one_send, one_recv, two_send, two_recv, out_sem,
):
    pools = ((pa0, pb0), (pa1, pb1), (pa2, pb2), (pa3, pb3))
    fars = ((fa0, fb0), (fa1, fb1), (fa2, fb2), (fa3, fb3))
    slots = ((ra0, rb0), (ra1, rb1), (ra2, rb2), (ra3, rb3))
    sends = ((sa0, sb0), (sa1, sb1), (sa0, sb0), (sa1, sb1))
    y = lax.axis_index("rows")
    col = lax.axis_index("cols")
    z, x, core = col // 8, (col // 2) % 4, col % 2

    def at(dy, dz, dx, dc):
        return (
            lax.rem(y + dy, 4),
            (lax.rem(z + dz, 4) * 4 + lax.rem(x + dx, 4)) * 2 + lax.rem(core + dc, 2),
        )

    def toward(st, way, flip):
        return at(0, way[st], way[1 - st], flip)

    def local(src, dst, sem):
        copy = pltpu.make_async_copy(src, dst, sem)
        copy.start()
        return copy

    def remote(src, dst, ssem, rsem, device):
        copy = pltpu.make_async_remote_copy(
            src_ref=src, dst_ref=dst, send_sem=ssem, recv_sem=rsem, device_id=device, device_id_type=MESH
        )
        copy.start()
        return copy

    own_pool = [
        local(
            theta.at[pl.ds(ph * 256 + st * 128, 128), pl.ds(b * 256, 256)],
            pools[ph][st].at[0, b],
            own_sem.at[ph, st, b],
        )
        for ph in range(2)
        for st in range(2)
        for b in range(4)
    ]

    barrier = pltpu.get_barrier_semaphore()
    partners = [(dy, 0, 0, 0) for dy in (1, 2, 3)] + [(0, 0, 0, 1)]
    partners += [(0, d, 0, dc) for d in (1, 3) for dc in (0, 1)]
    partners += [(0, 0, d, dc) for d in (1, 3) for dc in (0, 1)]
    for p in partners:
        pl.semaphore_signal(barrier, inc=1, device_id=at(*p), device_id_type=MESH)
    pl.semaphore_wait(barrier, len(partners))

    first = {}
    second = {}

    def held(ph, st, place):
        return fars[ph][st] if place == 5 else pools[ph][st].at[place]

    def chosen(ph, st, place, block):
        return fars[ph][st][block] if place == 5 else pools[ph][st][place, block]

    def hop(ph, i):
        for st in range(2):
            src, way = HOPS[i]
            if src:
                first[ph, st, src - 1].wait_recv()
            first[ph, st, i] = remote(
                held(ph, st, src), held(ph, st, i + 1), one_send.at[ph, st, i], one_recv.at[ph, st, i], toward(st, way, 0)
            )

    def hop_one(ph):
        hop(ph, 0)
        hop(ph, 1)

    def hop_two(ph):
        hop(ph, 2)
        hop(ph, 3)

    def look(way, flip):
        jobs = []
        for st in range(2):
            for there, f, places, start in PARTS:
                if (there[st], there[1 - st]) == way and f == flip:
                    jobs += [
                        (st * 32 + start + i, toward(st, tuple((4 - o) % 4 for o in INNER[place]), 0)[1])
                        for i, place in enumerate(places)
                    ]
        other = at(0, way[0], way[1], flip)[1]

        def entry(i, found):
            for k in range(20):
                n = col_nbrs[k, other * 4 + i]
                owner, block = n // 4, n % 4
                found = tuple(jnp.where(owner == j[1], block, f) for j, f in zip(jobs, found))
            return found

        found = lax.fori_loop(0, 4, entry, (jnp.int32(0),) * len(jobs))
        for j, f in zip(jobs, found):
            wanted[j[0]] = f

    def serve(ph, parts):
        for st in range(2):
            out, here = sends[ph][st], slots[ph][st]
            for m in parts:
                way, flip, places, start = PARTS[m]
                if ph >= 2:
                    second[ph - 2, st, m].wait_send()
                for i, place in enumerate(places):
                    out[start + i] = chosen(ph, st, place, wanted[st * 32 + start + i])
                part = pl.ds(start, len(places))
                second[ph, st, m] = remote(
                    out.at[part], here.at[part], two_send.at[ph, st, m], two_recv.at[ph, st, m], toward(st, way, flip)
                )

    def serve_one(ph):
        for st in range(2):
            first[ph, st, 3].wait_recv()
        serve(ph, (2, 3, 4, 5, 6, 7, 0, 1))

    def serve_two(ph):
        for st in range(2):
            first[ph, st, 4].wait_recv()
        serve(ph, (8, 10, 9, 11, SIBLING))
        for st in range(2):
            here = slots[ph][st]
            start = PARTS[SELF][3]
            for i, place in enumerate(PARTS[SELF][2]):
                here[start + i] = chosen(ph, st, place, wanted[st * 32 + start + i])
            for b in range(4):
                here[OWN + b] = pools[ph][st][0, b]

    def arrived(ph):
        for st in range(2):
            for m in range(SIBLING + 1):
                second[ph, st, m].wait_recv()

    def right(ph, c):
        here_a, here_b = slots[ph]
        total = None
        for k in range(20):
            e = c * 20 + k
            lhs = jnp.concatenate([here_a[index[e]], here_b[index[80 + e]]], axis=0)
            part = lax.dot_general(lhs, weights[e], (((1,), (1,)), ((), ())), preferred_element_type=F32)
            total = part if total is None else total + part
        return total

    def left(gathered, p):
        total = None
        for k in range(3):
            n = row_nbrs[k, 2 * y + p]
            part = jnp.dot(row_weights[p * 3 + k], gathered[n], preferred_element_type=F32)
            total = part if total is None else total + part
        return total

    for copy in own_pool:
        copy.wait()
    hop_one(0)
    hop_one(1)
    ys = [
        remote(
            sigma.at[pl.ds(half * 256, 256)],
            gathered_s.at[2 * y + half],
            ys_send.at[half, d - 1],
            ys_recv.at[half, d - 1],
            at(d, 0, 0, 0),
        )
        for half in range(2)
        for d in (1, 3, 2)
    ]
    loads = [
        local(sigma.at[pl.ds(half * 256, 256)], gathered_s.at[2 * y + half], own_sem.at[2, half, 0])
        for half in range(2)
    ]
    loads += [local(row_vals.at[2 * y + p], row_weights.at[pl.ds(p * 3, 3)], rv_sem.at[p]) for p in range(2)]
    loads += [local(col_vals.at[c], weights.at[pl.ds(c * 20, 20)], w_sem.at[c]) for c in range(4)]

    for way in ((1, 0), (0, 1)):
        for flip in range(2):
            look(way, flip)
    hop_two(0)
    for way in ((3, 0), (0, 3)):
        for flip in range(2):
            look(way, flip)
    hop_two(1)
    hop(0, 4)
    serve_one(0)
    for flip in range(2):
        look((0, 0), flip)
    serve_two(0)
    hop(1, 4)
    serve_one(1)
    serve_two(1)

    slot_of = slot_table()
    for dz in range(4):
        for dx in range(4):
            for flip in range(2):
                owner = at(0, (4 - dz) % 4, (4 - dx) % 4, flip)[1]
                table[owner] = slot_of[(dz, dx), flip]
                table[32 + owner] = slot_of[(dx, dz), flip]

    def place_of(c, carry):
        for k in range(20):
            n = col_nbrs[k, col * 4 + c]
            owner, block = n // 4, n % 4
            extra = jnp.where(owner == col, block, 0)
            index[c * 20 + k] = table[owner] + extra
            index[80 + c * 20 + k] = table[32 + owner] + extra
        return carry

    lax.fori_loop(0, 4, place_of, 0)

    for copy in loads:
        copy.wait()
    for copy in ys:
        copy.wait_recv()
    for p in range(2):
        panel = left(gathered_s, p).astype(BF16)
        for st in range(2):
            for b in range(4):
                pools[2 + p][st][0, b] = panel[st * 128 : (st + 1) * 128, b * 256 : (b + 1) * 256]
        hop_one(2 + p)

    yt = []

    def right_theta(half):
        arrived(half)

        def one(c, carry):
            cols = pl.ds(pl.multiple_of(c * 256, 256), 256)
            gathered_t[2 * y + half, :, cols] = right(half, c).astype(BF16)
            return carry

        lax.fori_loop(0, 4, one, 0)
        for d in (1, 3, 2):
            yt.append(
                remote(
                    gathered_t.at[2 * y + half],
                    gathered_t.at[2 * y + half],
                    yt_send.at[half, d - 1],
                    yt_recv.at[half, d - 1],
                    at(d, 0, 0, 0),
                )
            )

    right_theta(0)
    hop_two(2)
    hop_two(3)
    right_theta(1)
    hop(2, 4)
    serve_one(2)
    serve_two(2)
    hop(3, 4)
    serve_one(3)
    serve_two(3)

    outs = []

    def write(src, dst, rows, cols, sem):
        return pltpu.make_async_copy(src, dst.at[rows, cols], sem)

    top, low = pl.ds(0, 256), pl.ds(256, 256)

    arrived(2)

    def right_top(c, carry):
        total_s[0, c] = right(2, c)
        return carry

    lax.fori_loop(0, 4, right_top, 0)
    for copy in yt:
        copy.wait_recv()
    for p in range(2):
        both_cols = left(gathered_t, p)
        for c in range(4):
            total_t[p, c] = both_cols[:, c * 256 : (c + 1) * 256]
    scale_rows = jnp.sqrt(jnp.concatenate([column(var_rows[:, 0:128]), column(var_rows[:, 128:256])], axis=0))

    def finish(c, carry):
        cols = pl.ds(pl.multiple_of(c * 256, 256), 256)
        scale = scale_rows * jnp.sqrt(var_cols[:, cols])
        total_s[0, c], total_t[0, c] = both(total_s[0, c], total_t[0, c], scale)
        return carry

    lax.fori_loop(0, 4, finish, 0)
    for c in range(4):
        cols = pl.ds(c * 256, 256)
        outs.append(write(total_s.at[0, c], part_s, top, cols, out_sem.at[0, c]))
        outs.append(write(total_t.at[0, c], part_t, top, cols, out_sem.at[1, c]))
        outs.append(write(total_t.at[1, c], part_t, low, cols, out_sem.at[2, c]))
    for copy in outs:
        copy.start()

    arrived(3)

    def right_low(c, carry):
        cols = pl.ds(pl.multiple_of(c * 256, 256), 256)
        total_s[1, c] = right(3, c)
        write(total_s.at[1, c], part_s, low, cols, out_sem.at[3, c]).start()
        return carry

    lax.fori_loop(0, 4, right_low, 0)
    for c in range(4):
        outs.append(write(total_s.at[1, c], part_s, low, pl.ds(c * 256, 256), out_sem.at[3, c]))

    for copy in ys + yt:
        copy.wait_send()
    for copy in first.values():
        copy.wait_send()
    for (ph, st, j), copy in second.items():
        if ph >= 2:
            copy.wait_send()
    for copy in outs:
        copy.wait()


def update(var_rows, var_cols, part_s, part_t, nngp, ntk, s_in, t_in, n_out, k_out, s_top, t_top, in_sem, out_sem, top_in, top_out):
    rows = 32
    parts = 256 // rows
    loads = []
    for i in range(parts):
        for j, (src, dst) in enumerate(((part_s, s_in), (part_t, t_in))):
            loads.append(pltpu.make_async_copy(src.at[pl.ds(256 + i * rows, rows)], dst.at[i], in_sem.at[i, j]))
    tops, stores = [], []
    for i in range(2):
        for j, (src, mid, dst) in enumerate(((part_s, s_top, nngp), (part_t, t_top, ntk))):
            here = pl.ds(i * 128, 128)
            tops.append(
                (
                    pltpu.make_async_copy(src.at[here], mid.at[i], top_in.at[i, j]),
                    pltpu.make_async_copy(mid.at[i], dst.at[here], top_out.at[i, j]),
                )
            )
    for copy in loads:
        copy.start()
    for copy, _ in tops:
        copy.start()
    scale_cols = jnp.sqrt(var_cols[...])
    for i in range(parts):
        first, lane = i * rows % 128, 256 + i * rows // 128 * 128
        scale = jnp.sqrt(column(var_rows[:, lane : lane + 128])[first : first + rows]) * scale_cols
        loads[2 * i].wait()
        loads[2 * i + 1].wait()
        n_out[i], k_out[i] = both(s_in[i], t_in[i], scale)
        for j, (src, dst) in enumerate(((n_out, nngp), (k_out, ntk))):
            copy = pltpu.make_async_copy(src.at[i], dst.at[pl.ds(256 + i * rows, rows)], out_sem.at[i, j])
            copy.start()
            stores.append(copy)
        if i % 2 and i // 2 < len(tops):
            there, back = tops[i // 2]
            there.wait()
            back.start()
            stores.append(back)
    for copy in stores:
        copy.wait()


def shards(sigma_in, theta_in, var_rows, var_cols, row_nbrs, row_vals, col_nbrs, col_vals):
    smem = pl.BlockSpec(memory_space=pltpu.SMEM)
    hbm = pl.BlockSpec(memory_space=pl.ANY)
    dma = pltpu.SemaphoreType.DMA
    out = jax.ShapeDtypeStruct((512, 1024), F32)
    vmem = pl.BlockSpec(memory_space=pltpu.VMEM)
    var_rows, var_cols = var_rows.reshape(1, 512), var_cols.reshape(1, 1024)
    part_s, part_t = pl.pallas_call(
        kernel,
        out_shape=(out, out),
        in_specs=[smem, smem, vmem, vmem, hbm, hbm, hbm, hbm],
        out_specs=(hbm, hbm),
        scratch_shapes=[
            pltpu.SMEM((64,), jnp.int32),
            pltpu.SMEM((64,), jnp.int32),
            pltpu.SMEM((160,), jnp.int32),
            pltpu.VMEM((80, 256, 256), BF16),
            pltpu.VMEM((6, 256, 256), BF16),
            pltpu.VMEM((8, 256, 1024), BF16),
            pltpu.VMEM((8, 256, 1024), BF16),
            pltpu.VMEM((2, 4, 256, 256), F32),
            pltpu.VMEM((2, 4, 256, 256), F32),
        ]
        + [pltpu.VMEM((5, 4, 128, 256), BF16)] * 8
        + [pltpu.VMEM((4, 128, 256), BF16)] * 8
        + [pltpu.VMEM((SLOTS, 128, 256), BF16)] * 8
        + [pltpu.VMEM((26, 128, 256), BF16)] * 4
        + [
            dma((4,)),
            dma((2,)),
            dma((3, 2, 4)),
            dma((2, 3)),
            dma((2, 3)),
            dma((2, 3)),
            dma((2, 3)),
            dma((4, 2, 5)),
            dma((4, 2, 5)),
            dma((4, 2, 13)),
            dma((4, 2, 13)),
            dma((4, 4)),
        ],
        compiler_params=pltpu.CompilerParams(
            collective_id=0, has_side_effects=True, vmem_limit_bytes=62 * 1024 * 1024
        ),
    )(col_nbrs.T, row_nbrs.T, var_rows, var_cols, theta_in, sigma_in, row_vals, col_vals)

    return pl.pallas_call(
        update,
        out_shape=(out, out),
        in_specs=[vmem, vmem, hbm, hbm],
        out_specs=(hbm, hbm),
        scratch_shapes=[pltpu.VMEM((8, 32, 1024), F32)] * 4
        + [pltpu.VMEM((2, 128, 1024), F32)] * 2
        + [dma((8, 2)), dma((8, 2)), dma((2, 2)), dma((2, 2))],
        compiler_params=pltpu.CompilerParams(vmem_limit_bytes=62 * 1024 * 1024),
    )(var_rows, var_cols, part_s, part_t)


def solution(mesh):
    in_specs = (
        P("rows", "cols"),
        P("rows", "cols"),
        P("rows"),
        P("cols"),
        P(),
        P(),
        P(),
        P("cols", None, None, None),
    )
    out_specs = (P("rows", "cols"), P("rows", "cols"))
    return jax.shard_map(shards, mesh=mesh, in_specs=in_specs, out_specs=out_specs, check_vma=False)
```

```python
import functools
import math

import jax
import jax.numpy as jnp
from jax import lax
from jax.experimental import pallas as pl
from jax.experimental.pallas import tpu as pltpu
from jax.sharding import PartitionSpec as P

MESH = pl.DeviceIdType.MESH
BF16 = jnp.bfloat16
F32 = jnp.float32

ATAN = (
    0.9999998979,
    -0.3333196033,
    0.1996924122,
    -0.1401660921,
    0.09906147193,
    -0.05936764426,
    0.02416647519,
    -0.004668829048,
)


INNER = ((0, 0), (0, 1), (0, 3), (1, 1), (3, 3), (2, 1))
HOPS = ((0, (0, 1)), (0, (0, 3)), (1, (1, 0)), (2, (3, 0)), (3, (1, 0)))
OUTER = (((1, 0), (2,)), ((3, 0), (4, 0, 1)), ((0, 1), (1, 3, 5)), ((0, 3), (3, 5, 4)))
PARTS = []
for way, places in OUTER:
    for flip in (0, 1):
        PARTS.append((way, flip, places, sum(len(p[2]) for p in PARTS)))
PARTS.append(((0, 0), 1, (0, 1, 2, 3, 4, 5), 20))
PARTS.append(((0, 0), 0, (1, 2, 3, 4, 5), 26))
SIBLING, SELF = 8, 9
OWN = 31
SLOTS = 35


def slot_table():
    table = {}
    for way, flip, places, start in PARTS:
        for i, p in enumerate(places):
            offset = tuple((a + b) % 4 for a, b in zip(INNER[p], way))
            table[offset, flip] = start + i
    table[(0, 0), 0] = OWN
    return table


def arc(t):
    t2 = t * t
    total = jnp.full_like(t, ATAN[-1])
    for c in ATAN[-2::-1]:
        total = total * t2 + c
    return total * t


def column(row):
    place = [lax.broadcasted_iota(jnp.int32, (128, 128), i) for i in range(2)]
    return jnp.sum(jnp.where(place[0] == place[1], row, 0.0), axis=1, keepdims=True)


def both(a, t, scale):
    square = scale * scale + a * a
    inverse = lax.rsqrt(square)
    angle = arc(a / (scale + square * inverse))
    share = 0.5 + angle * (2 / math.pi)
    kern = scale * (scale * inverse * (1 / math.pi) + share * (a * inverse))
    return kern, kern + t * share


def kernel(
    col_hbm, row_nbrs, var_rows_hbm, var_cols_hbm, theta, sigma, row_vals, col_vals,
    part_s, part_t,
    col_nbrs, var_rows, var_cols, wanted, table, index, weights, row_weights, gathered_s, gathered_t, total_s, total_t,
    pa0, pa1, pa2, pa3, pb0, pb1, pb2, pb3,
    fa0, fa1, fa2, fa3, fb0, fb1, fb2, fb3,
    ra0, ra1, ra2, ra3, rb0, rb1, rb2, rb3,
    sa0, sa1, sb0, sb1,
    w_sem, rv_sem, own_sem, ys_send, ys_recv, yt_send, yt_recv,
    one_send, one_recv, two_send, two_recv, out_sem, small_sem,
):
    pools = ((pa0, pb0), (pa1, pb1), (pa2, pb2), (pa3, pb3))
    fars = ((fa0, fb0), (fa1, fb1), (fa2, fb2), (fa3, fb3))
    slots = ((ra0, rb0), (ra1, rb1), (ra2, rb2), (ra3, rb3))
    sends = ((sa0, sb0), (sa1, sb1), (sa0, sb0), (sa1, sb1))
    y = lax.axis_index("rows")
    col = lax.axis_index("cols")
    z, x, core = col // 8, (col // 2) % 4, col % 2

    def at(dy, dz, dx, dc):
        return (
            lax.rem(y + dy, 4),
            (lax.rem(z + dz, 4) * 4 + lax.rem(x + dx, 4)) * 2 + lax.rem(core + dc, 2),
        )

    def toward(st, way, flip):
        return at(0, way[st], way[1 - st], flip)

    def local(src, dst, sem):
        copy = pltpu.make_async_copy(src, dst, sem)
        copy.start()
        return copy

    def remote(src, dst, ssem, rsem, device):
        copy = pltpu.make_async_remote_copy(
            src_ref=src, dst_ref=dst, send_sem=ssem, recv_sem=rsem, device_id=device, device_id_type=MESH
        )
        copy.start()
        return copy

    own_pool = [
        local(
            theta.at[pl.ds(ph * 256 + st * 128, 128), pl.ds(b * 256, 256)],
            pools[ph][st].at[0, b],
            own_sem.at[ph, st, b],
        )
        for ph in range(2)
        for st in range(2)
        for b in range(4)
    ]

    smalls = [
        local(src, dst, small_sem.at[i])
        for i, (src, dst) in enumerate(((col_hbm, col_nbrs), (var_rows_hbm, var_rows), (var_cols_hbm, var_cols)))
    ]

    barrier = pltpu.get_barrier_semaphore()
    partners = [(dy, 0, 0, 0) for dy in (1, 2, 3)] + [(0, 0, 0, 1)]
    partners += [(0, d, 0, dc) for d in (1, 3) for dc in (0, 1)]
    partners += [(0, 0, d, dc) for d in (1, 3) for dc in (0, 1)]
    for p in partners:
        pl.semaphore_signal(barrier, inc=1, device_id=at(*p), device_id_type=MESH)
    pl.semaphore_wait(barrier, len(partners))

    first = {}
    second = {}

    def held(ph, st, place):
        return fars[ph][st] if place == 5 else pools[ph][st].at[place]

    def chosen(ph, st, place, block):
        return fars[ph][st][block] if place == 5 else pools[ph][st][place, block]

    def hop(ph, i):
        for st in range(2):
            src, way = HOPS[i]
            if src:
                first[ph, st, src - 1].wait_recv()
            first[ph, st, i] = remote(
                held(ph, st, src), held(ph, st, i + 1), one_send.at[ph, st, i], one_recv.at[ph, st, i], toward(st, way, 0)
            )

    def hop_one(ph):
        hop(ph, 0)
        hop(ph, 1)

    def hop_two(ph):
        hop(ph, 2)
        hop(ph, 3)

    def look(way, flip):
        jobs = []
        for st in range(2):
            for there, f, places, start in PARTS:
                if (there[st], there[1 - st]) == way and f == flip:
                    jobs += [
                        (st * 32 + start + i, toward(st, tuple((4 - o) % 4 for o in INNER[place]), 0)[1])
                        for i, place in enumerate(places)
                    ]
        other = at(0, way[0], way[1], flip)[1]

        def entry(i, found):
            for k in range(20):
                n = col_nbrs[k, other * 4 + i]
                owner, block = n // 4, n % 4
                found = tuple(jnp.where(owner == j[1], block, f) for j, f in zip(jobs, found))
            return found

        found = lax.fori_loop(0, 4, entry, (jnp.int32(0),) * len(jobs))
        for j, f in zip(jobs, found):
            wanted[j[0]] = f

    def serve(ph, parts):
        for st in range(2):
            out, here = sends[ph][st], slots[ph][st]
            for m in parts:
                way, flip, places, start = PARTS[m]
                if ph >= 2:
                    second[ph - 2, st, m].wait_send()
                for i, place in enumerate(places):
                    out[start + i] = chosen(ph, st, place, wanted[st * 32 + start + i])
                part = pl.ds(start, len(places))
                second[ph, st, m] = remote(
                    out.at[part], here.at[part], two_send.at[ph, st, m], two_recv.at[ph, st, m], toward(st, way, flip)
                )

    def serve_one(ph):
        for st in range(2):
            first[ph, st, 3].wait_recv()
        serve(ph, (2, 3, 0, 1))

    def serve_two(ph):
        for st in range(2):
            first[ph, st, 4].wait_recv()
        serve(ph, (4, 6, 5, 7, SIBLING))
        for st in range(2):
            here = slots[ph][st]
            start = PARTS[SELF][3]
            for i, place in enumerate(PARTS[SELF][2]):
                here[start + i] = chosen(ph, st, place, wanted[st * 32 + start + i])
            for b in range(4):
                here[OWN + b] = pools[ph][st][0, b]

    def arrived(ph):
        for st in range(2):
            for m in range(SIBLING + 1):
                second[ph, st, m].wait_recv()

    def right(ph, c):
        here_a, here_b = slots[ph]
        total = None
        for k in range(20):
            e = c * 20 + k
            lhs = jnp.concatenate([here_a[index[e]], here_b[index[80 + e]]], axis=0)
            part = lax.dot_general(lhs, weights[e], (((1,), (1,)), ((), ())), preferred_element_type=F32)
            total = part if total is None else total + part
        return total

    def left(gathered, p):
        total = None
        for k in range(3):
            n = row_nbrs[k, 2 * y + p]
            part = jnp.dot(row_weights[p * 3 + k], gathered[n], preferred_element_type=F32)
            total = part if total is None else total + part
        return total

    for copy in own_pool:
        copy.wait()
    hop_one(0)
    hop_one(1)
    ys = [
        remote(
            sigma.at[pl.ds(half * 256, 256)],
            gathered_s.at[2 * y + half],
            ys_send.at[half, d - 1],
            ys_recv.at[half, d - 1],
            at(d, 0, 0, 0),
        )
        for half in range(2)
        for d in (1, 3, 2)
    ]
    loads = [
        local(sigma.at[pl.ds(half * 256, 256)], gathered_s.at[2 * y + half], own_sem.at[2, half, 0])
        for half in range(2)
    ]
    loads += [local(row_vals.at[2 * y + p], row_weights.at[pl.ds(p * 3, 3)], rv_sem.at[p]) for p in range(2)]
    loads += [local(col_vals.at[c], weights.at[pl.ds(c * 20, 20)], w_sem.at[c]) for c in range(4)]

    for copy in smalls:
        copy.wait()
    for way in ((1, 0), (0, 1)):
        for flip in range(2):
            look(way, flip)
    hop_two(0)
    for way in ((3, 0), (0, 3)):
        for flip in range(2):
            look(way, flip)
    hop_two(1)
    hop(0, 4)
    serve_one(0)
    hop(1, 4)
    serve_one(1)
    for flip in range(2):
        look((0, 0), flip)
    serve_two(0)
    serve_two(1)

    slot_of = slot_table()
    for dz in range(4):
        for dx in range(4):
            for flip in range(2):
                owner = at(0, (4 - dz) % 4, (4 - dx) % 4, flip)[1]
                table[owner] = slot_of[(dz, dx), flip]
                table[32 + owner] = slot_of[(dx, dz), flip]

    def place_of(c, carry):
        for k in range(20):
            n = col_nbrs[k, col * 4 + c]
            owner, block = n // 4, n % 4
            extra = jnp.where(owner == col, block, 0)
            index[c * 20 + k] = table[owner] + extra
            index[80 + c * 20 + k] = table[32 + owner] + extra
        return carry

    lax.fori_loop(0, 4, place_of, 0)

    for copy in loads:
        copy.wait()
    for copy in ys:
        copy.wait_recv()
    for p in range(2):
        panel = left(gathered_s, p).astype(BF16)
        for st in range(2):
            for b in range(4):
                pools[2 + p][st][0, b] = panel[st * 128 : (st + 1) * 128, b * 256 : (b + 1) * 256]
        hop_one(2 + p)

    yt = []

    def right_theta(half):
        arrived(half)

        def one(c, carry):
            cols = pl.ds(pl.multiple_of(c * 256, 256), 256)
            gathered_t[2 * y + half, :, cols] = right(half, c).astype(BF16)
            return carry

        lax.fori_loop(0, 4, one, 0)
        for d in (1, 3, 2):
            yt.append(
                remote(
                    gathered_t.at[2 * y + half],
                    gathered_t.at[2 * y + half],
                    yt_send.at[half, d - 1],
                    yt_recv.at[half, d - 1],
                    at(d, 0, 0, 0),
                )
            )

    right_theta(0)
    hop_two(2)
    hop_two(3)
    right_theta(1)
    hop(2, 4)
    serve_one(2)
    hop(3, 4)
    serve_two(2)
    serve_one(3)
    serve_two(3)

    outs = []

    def write(src, dst, rows, cols, sem):
        return pltpu.make_async_copy(src, dst.at[rows, cols], sem)

    top, low = pl.ds(0, 256), pl.ds(256, 256)

    arrived(2)

    def right_top(c, carry):
        total_s[0, c] = right(2, c)
        return carry

    lax.fori_loop(0, 4, right_top, 0)
    for copy in yt:
        copy.wait_recv()
    for p in range(2):
        both_cols = left(gathered_t, p)
        for c in range(4):
            total_t[p, c] = both_cols[:, c * 256 : (c + 1) * 256]

    def scale_of(half, cols):
        parts = [column(var_rows[:, half * 256 + i : half * 256 + i + 128]) for i in (0, 128)]
        return jnp.sqrt(jnp.concatenate(parts, axis=0)) * jnp.sqrt(var_cols[:, cols])

    def finish(c, carry):
        cols = pl.ds(pl.multiple_of(c * 256, 256), 256)
        total_s[0, c], total_t[0, c] = both(total_s[0, c], total_t[0, c], scale_of(0, cols))
        return carry

    lax.fori_loop(0, 4, finish, 0)
    for c in range(4):
        cols = pl.ds(c * 256, 256)
        outs.append(write(total_s.at[0, c], part_s, top, cols, out_sem.at[0, c]))
        outs.append(write(total_t.at[0, c], part_t, top, cols, out_sem.at[1, c]))
    for copy in outs:
        copy.start()

    arrived(3)
    scale_rows = scale_of(1, pl.ds(0, 1024))
    for c in range(4):
        cols = pl.ds(c * 256, 256)
        total_s[1, c], total_t[1, c] = both(right(3, c), total_t[1, c], scale_rows[:, c * 256 : (c + 1) * 256])
        for i, (src, dst) in enumerate(((total_s, part_s), (total_t, part_t))):
            outs.append(write(src.at[1, c], dst, low, cols, out_sem.at[2 + i, c]))
            outs[-1].start()

    for copy in ys + yt:
        copy.wait_send()
    for copy in first.values():
        copy.wait_send()
    for (ph, st, j), copy in second.items():
        if ph >= 2:
            copy.wait_send()
    for copy in outs:
        copy.wait()


def update(part_s, part_t, nngp, ntk, held, in_sem, out_sem):
    copies = []
    for i in range(4):
        rows = pl.ds(i * 128, 128)
        for j, (src, dst) in enumerate(((part_s, nngp), (part_t, ntk))):
            copies.append(
                (
                    pltpu.make_async_copy(src.at[rows], held.at[i, j], in_sem.at[i, j]),
                    pltpu.make_async_copy(held.at[i, j], dst.at[rows], out_sem.at[i, j]),
                )
            )
    for there, _ in copies:
        there.start()
    for there, back in copies:
        there.wait()
        back.start()
    for _, back in copies:
        back.wait()


def shards(sigma_in, theta_in, var_rows, var_cols, row_nbrs, row_vals, col_nbrs, col_vals):
    smem = pl.BlockSpec(memory_space=pltpu.SMEM)
    hbm = pl.BlockSpec(memory_space=pl.ANY)
    dma = pltpu.SemaphoreType.DMA
    out = jax.ShapeDtypeStruct((512, 1024), F32)
    vmem = pl.BlockSpec(memory_space=pltpu.VMEM)
    var_rows, var_cols = var_rows.reshape(1, 512), var_cols.reshape(1, 1024)
    part_s, part_t = pl.pallas_call(
        kernel,
        out_shape=(out, out),
        in_specs=[hbm, smem, hbm, hbm, hbm, hbm, hbm, hbm],
        out_specs=(hbm, hbm),
        scratch_shapes=[
            pltpu.SMEM((20, 128), jnp.int32),
            pltpu.VMEM((1, 512), F32),
            pltpu.VMEM((1, 1024), F32),
            pltpu.SMEM((64,), jnp.int32),
            pltpu.SMEM((64,), jnp.int32),
            pltpu.SMEM((160,), jnp.int32),
            pltpu.VMEM((80, 256, 256), BF16),
            pltpu.VMEM((6, 256, 256), BF16),
            pltpu.VMEM((8, 256, 1024), BF16),
            pltpu.VMEM((8, 256, 1024), BF16),
            pltpu.VMEM((2, 4, 256, 256), F32),
            pltpu.VMEM((2, 4, 256, 256), F32),
        ]
        + [pltpu.VMEM((5, 4, 128, 256), BF16)] * 8
        + [pltpu.VMEM((4, 128, 256), BF16)] * 8
        + [pltpu.VMEM((SLOTS, 128, 256), BF16)] * 8
        + [pltpu.VMEM((26, 128, 256), BF16)] * 4
        + [
            dma((4,)),
            dma((2,)),
            dma((3, 2, 4)),
            dma((2, 3)),
            dma((2, 3)),
            dma((2, 3)),
            dma((2, 3)),
            dma((4, 2, 5)),
            dma((4, 2, 5)),
            dma((4, 2, 9)),
            dma((4, 2, 9)),
            dma((4, 4)),
            dma((3,)),
        ],
        compiler_params=pltpu.CompilerParams(
            collective_id=0, has_side_effects=True, vmem_limit_bytes=62 * 1024 * 1024
        ),
    )(col_nbrs.T, row_nbrs.T, var_rows, var_cols, theta_in, sigma_in, row_vals, col_vals)

    return pl.pallas_call(
        update,
        out_shape=(out, out),
        in_specs=[hbm, hbm],
        out_specs=(hbm, hbm),
        scratch_shapes=[pltpu.VMEM((4, 2, 128, 1024), F32), dma((4, 2)), dma((4, 2))],
        compiler_params=pltpu.CompilerParams(vmem_limit_bytes=62 * 1024 * 1024),
    )(part_s, part_t)


def solution(mesh):
    in_specs = (
        P("rows", "cols"),
        P("rows", "cols"),
        P("rows"),
        P("cols"),
        P(),
        P(),
        P(),
        P("cols", None, None, None),
    )
    out_specs = (P("rows", "cols"), P("rows", "cols"))
    return jax.shard_map(shards, mesh=mesh, in_specs=in_specs, out_specs=out_specs, check_vma=False)
```

```python
import functools
import math

import jax
import jax.numpy as jnp
from jax import lax
from jax.experimental import pallas as pl
from jax.experimental.pallas import tpu as pltpu
from jax.sharding import PartitionSpec as P

MESH = pl.DeviceIdType.MESH
BF16 = jnp.bfloat16
F32 = jnp.float32

ATAN = (
    0.9999998979,
    -0.3333196033,
    0.1996924122,
    -0.1401660921,
    0.09906147193,
    -0.05936764426,
    0.02416647519,
    -0.004668829048,
)


INNER = ((0, 0), (0, 1), (0, 3), (1, 1), (3, 3), (2, 1))
HOPS = ((0, (0, 1)), (0, (0, 3)), (1, (1, 0)), (2, (3, 0)), (3, (1, 0)))
OUTER = (((1, 0), (2,)), ((3, 0), (4, 0, 1)), ((0, 1), (1, 3, 5)), ((0, 3), (3, 5, 4)))
PARTS = []
for way, places in OUTER:
    for flip in (0, 1):
        PARTS.append((way, flip, places, sum(len(p[2]) for p in PARTS)))
PARTS.append(((0, 0), 1, (0, 1, 2, 3, 4, 5), 20))
PARTS.append(((0, 0), 0, (1, 2, 3, 4, 5), 26))
SIBLING, SELF = 8, 9
OWN = 31
SLOTS = 35


def slot_table():
    table = {}
    for way, flip, places, start in PARTS:
        for i, p in enumerate(places):
            offset = tuple((a + b) % 4 for a, b in zip(INNER[p], way))
            table[offset, flip] = start + i
    table[(0, 0), 0] = OWN
    return table


def arc(t):
    t2 = t * t
    total = jnp.full_like(t, ATAN[-1])
    for c in ATAN[-2::-1]:
        total = total * t2 + c
    return total * t


def column(row):
    place = [lax.broadcasted_iota(jnp.int32, (128, 128), i) for i in range(2)]
    return jnp.sum(jnp.where(place[0] == place[1], row, 0.0), axis=1, keepdims=True)


def both(a, t, scale):
    square = scale * scale + a * a
    inverse = lax.rsqrt(square)
    angle = arc(a / (scale + square * inverse))
    share = 0.5 + angle * (2 / math.pi)
    kern = scale * (scale * inverse * (1 / math.pi) + share * (a * inverse))
    return kern, kern + t * share


def kernel(
    col_hbm, row_nbrs, var_rows_hbm, var_cols_hbm, theta, sigma, row_vals, col_vals,
    part_s, part_t,
    col_nbrs, var_rows, var_cols, wanted, table, index, weights, row_weights, gathered_s, gathered_t, total_s, total_t,
    pa0, pa1, pa2, pa3, pb0, pb1, pb2, pb3,
    fa0, fa1, fa2, fa3, fb0, fb1, fb2, fb3,
    ra0, ra1, ra2, ra3, rb0, rb1, rb2, rb3,
    sa0, sa1, sb0, sb1,
    w_sem, rv_sem, own_sem, ys_send, ys_recv, yt_send, yt_recv,
    one_send, one_recv, two_send, two_recv, out_sem, small_sem,
):
    pools = ((pa0, pb0), (pa1, pb1), (pa2, pb2), (pa3, pb3))
    fars = ((fa0, fb0), (fa1, fb1), (fa2, fb2), (fa3, fb3))
    slots = ((ra0, rb0), (ra1, rb1), (ra2, rb2), (ra3, rb3))
    sends = ((sa0, sb0), (sa1, sb1), (sa0, sb0), (sa1, sb1))
    y = lax.axis_index("rows")
    col = lax.axis_index("cols")
    z, x, core = col // 8, (col // 2) % 4, col % 2

    def at(dy, dz, dx, dc):
        return (
            lax.rem(y + dy, 4),
            (lax.rem(z + dz, 4) * 4 + lax.rem(x + dx, 4)) * 2 + lax.rem(core + dc, 2),
        )

    def toward(st, way, flip):
        return at(0, way[st], way[1 - st], flip)

    def local(src, dst, sem):
        copy = pltpu.make_async_copy(src, dst, sem)
        copy.start()
        return copy

    def remote(src, dst, ssem, rsem, device):
        copy = pltpu.make_async_remote_copy(
            src_ref=src, dst_ref=dst, send_sem=ssem, recv_sem=rsem, device_id=device, device_id_type=MESH
        )
        copy.start()
        return copy

    own_pool = [
        local(
            theta.at[pl.ds(ph * 256 + st * 128, 128), pl.ds(b * 256, 256)],
            pools[ph][st].at[0, b],
            own_sem.at[ph, st, b],
        )
        for ph in range(2)
        for st in range(2)
        for b in range(4)
    ]

    smalls = [
        local(src, dst, small_sem.at[i])
        for i, (src, dst) in enumerate(((col_hbm, col_nbrs), (var_rows_hbm, var_rows), (var_cols_hbm, var_cols)))
    ]

    barrier = pltpu.get_barrier_semaphore()
    partners = [(dy, 0, 0, 0) for dy in (1, 2, 3)] + [(0, 0, 0, 1)]
    partners += [(0, d, 0, dc) for d in (1, 3) for dc in (0, 1)]
    partners += [(0, 0, d, dc) for d in (1, 3) for dc in (0, 1)]
    for p in partners:
        pl.semaphore_signal(barrier, inc=1, device_id=at(*p), device_id_type=MESH)
    pl.semaphore_wait(barrier, len(partners))

    first = {}
    second = {}

    def held(ph, st, place):
        return fars[ph][st] if place == 5 else pools[ph][st].at[place]

    def chosen(ph, st, place, block):
        return fars[ph][st][block] if place == 5 else pools[ph][st][place, block]

    def hop(ph, i):
        for st in range(2):
            src, way = HOPS[i]
            if src:
                first[ph, st, src - 1].wait_recv()
            first[ph, st, i] = remote(
                held(ph, st, src), held(ph, st, i + 1), one_send.at[ph, st, i], one_recv.at[ph, st, i], toward(st, way, 0)
            )

    def hop_one(ph):
        hop(ph, 0)
        hop(ph, 1)

    def hop_two(ph):
        hop(ph, 2)
        hop(ph, 3)

    def look(way, flip):
        jobs = []
        for st in range(2):
            for there, f, places, start in PARTS:
                if (there[st], there[1 - st]) == way and f == flip:
                    jobs += [
                        (st * 32 + start + i, toward(st, tuple((4 - o) % 4 for o in INNER[place]), 0)[1])
                        for i, place in enumerate(places)
                    ]
        other = at(0, way[0], way[1], flip)[1]

        def entry(i, found):
            for k in range(20):
                n = col_nbrs[k, other * 4 + i]
                owner, block = n // 4, n % 4
                found = tuple(jnp.where(owner == j[1], block, f) for j, f in zip(jobs, found))
            return found

        found = lax.fori_loop(0, 4, entry, (jnp.int32(0),) * len(jobs))
        for j, f in zip(jobs, found):
            wanted[j[0]] = f

    def serve(ph, parts):
        for m in parts:
            for st in range(2):
                out, here = sends[ph][st], slots[ph][st]
                way, flip, places, start = PARTS[m]
                if ph >= 2:
                    second[ph - 2, st, m].wait_send()
                for i, place in enumerate(places):
                    out[start + i] = chosen(ph, st, place, wanted[st * 32 + start + i])
                part = pl.ds(start, len(places))
                second[ph, st, m] = remote(
                    out.at[part], here.at[part], two_send.at[ph, st, m], two_recv.at[ph, st, m], toward(st, way, flip)
                )

    def serve_one(ph):
        for st in range(2):
            first[ph, st, 3].wait_recv()
        serve(ph, (2, 3, 0, 1))

    def serve_two(ph):
        for st in range(2):
            first[ph, st, 4].wait_recv()
        serve(ph, (4, 6, 5, 7, SIBLING))
        for st in range(2):
            here = slots[ph][st]
            start = PARTS[SELF][3]
            for i, place in enumerate(PARTS[SELF][2]):
                here[start + i] = chosen(ph, st, place, wanted[st * 32 + start + i])
            for b in range(4):
                here[OWN + b] = pools[ph][st][0, b]

    def arrived(ph):
        for st in range(2):
            for m in range(SIBLING + 1):
                second[ph, st, m].wait_recv()

    def right(ph, c):
        here_a, here_b = slots[ph]
        total = None
        for k in range(20):
            e = c * 20 + k
            lhs = jnp.concatenate([here_a[index[e]], here_b[index[80 + e]]], axis=0)
            part = lax.dot_general(lhs, weights[e], (((1,), (1,)), ((), ())), preferred_element_type=F32)
            total = part if total is None else total + part
        return total

    def left(gathered, p):
        total = None
        for k in range(3):
            n = row_nbrs[k, 2 * y + p]
            part = jnp.dot(row_weights[p * 3 + k], gathered[n], preferred_element_type=F32)
            total = part if total is None else total + part
        return total

    for ph in range(2):
        for copy in own_pool[ph * 8 : ph * 8 + 8]:
            copy.wait()
        hop_one(ph)
    ys = [
        remote(
            sigma.at[pl.ds(half * 256, 256)],
            gathered_s.at[2 * y + half],
            ys_send.at[half, d - 1],
            ys_recv.at[half, d - 1],
            at(d, 0, 0, 0),
        )
        for half in range(2)
        for d in (1, 3, 2)
    ]
    loads = [
        local(sigma.at[pl.ds(half * 256, 256)], gathered_s.at[2 * y + half], own_sem.at[2, half, 0])
        for half in range(2)
    ]
    loads += [local(row_vals.at[2 * y + p], row_weights.at[pl.ds(p * 3, 3)], rv_sem.at[p]) for p in range(2)]
    loads += [local(col_vals.at[c], weights.at[pl.ds(c * 20, 20)], w_sem.at[c]) for c in range(4)]

    for copy in smalls:
        copy.wait()
    for way in ((1, 0), (0, 1)):
        for flip in range(2):
            look(way, flip)
    hop_two(0)
    for way in ((3, 0), (0, 3)):
        for flip in range(2):
            look(way, flip)
    hop_two(1)
    hop(0, 4)
    serve_one(0)
    hop(1, 4)
    serve_one(1)
    for flip in range(2):
        look((0, 0), flip)
    serve_two(0)
    serve_two(1)

    slot_of = slot_table()
    for dz in range(4):
        for dx in range(4):
            for flip in range(2):
                owner = at(0, (4 - dz) % 4, (4 - dx) % 4, flip)[1]
                table[owner] = slot_of[(dz, dx), flip]
                table[32 + owner] = slot_of[(dx, dz), flip]

    def place_of(c, carry):
        for k in range(20):
            n = col_nbrs[k, col * 4 + c]
            owner, block = n // 4, n % 4
            extra = jnp.where(owner == col, block, 0)
            index[c * 20 + k] = table[owner] + extra
            index[80 + c * 20 + k] = table[32 + owner] + extra
        return carry

    lax.fori_loop(0, 4, place_of, 0)

    for copy in loads:
        copy.wait()
    for copy in ys:
        copy.wait_recv()
    for p in range(2):
        panel = left(gathered_s, p).astype(BF16)
        for st in range(2):
            for b in range(4):
                pools[2 + p][st][0, b] = panel[st * 128 : (st + 1) * 128, b * 256 : (b + 1) * 256]
        hop_one(2 + p)

    yt = []

    def right_theta(half):
        arrived(half)

        def one(c, carry):
            cols = pl.ds(pl.multiple_of(c * 256, 256), 256)
            gathered_t[2 * y + half, :, cols] = right(half, c).astype(BF16)
            return carry

        lax.fori_loop(0, 4, one, 0)
        for d in (1, 3, 2):
            yt.append(
                remote(
                    gathered_t.at[2 * y + half],
                    gathered_t.at[2 * y + half],
                    yt_send.at[half, d - 1],
                    yt_recv.at[half, d - 1],
                    at(d, 0, 0, 0),
                )
            )

    right_theta(0)
    hop_two(2)
    hop_two(3)
    right_theta(1)
    hop(2, 4)
    serve_one(2)
    hop(3, 4)
    serve_two(2)
    serve_one(3)
    serve_two(3)

    outs = []

    def write(src, dst, rows, cols, sem):
        return pltpu.make_async_copy(src, dst.at[rows, cols], sem)

    top, low = pl.ds(0, 256), pl.ds(256, 256)

    arrived(2)

    def right_top(c, carry):
        total_s[0, c] = right(2, c)
        return carry

    lax.fori_loop(0, 4, right_top, 0)
    for copy in yt:
        copy.wait_recv()
    for p in range(2):
        both_cols = left(gathered_t, p)
        for c in range(4):
            total_t[p, c] = both_cols[:, c * 256 : (c + 1) * 256]

    def scale_of(half, cols):
        parts = [column(var_rows[:, half * 256 + i : half * 256 + i + 128]) for i in (0, 128)]
        return jnp.sqrt(jnp.concatenate(parts, axis=0)) * jnp.sqrt(var_cols[:, cols])

    def finish(c, carry):
        cols = pl.ds(pl.multiple_of(c * 256, 256), 256)
        total_s[0, c], total_t[0, c] = both(total_s[0, c], total_t[0, c], scale_of(0, cols))
        return carry

    lax.fori_loop(0, 4, finish, 0)
    for c in range(4):
        cols = pl.ds(c * 256, 256)
        outs.append(write(total_s.at[0, c], part_s, top, cols, out_sem.at[0, c]))
        outs.append(write(total_t.at[0, c], part_t, top, cols, out_sem.at[1, c]))
    for copy in outs:
        copy.start()

    arrived(3)
    scale_rows = scale_of(1, pl.ds(0, 1024))
    for c in range(4):
        cols = pl.ds(c * 256, 256)
        total_s[1, c], total_t[1, c] = both(right(3, c), total_t[1, c], scale_rows[:, c * 256 : (c + 1) * 256])
        for i, (src, dst) in enumerate(((total_s, part_s), (total_t, part_t))):
            outs.append(write(src.at[1, c], dst, low, cols, out_sem.at[2 + i, c]))
            outs[-1].start()

    for copy in ys + yt:
        copy.wait_send()
    for copy in first.values():
        copy.wait_send()
    for (ph, st, j), copy in second.items():
        if ph >= 2:
            copy.wait_send()
    for copy in outs:
        copy.wait()


def update(part_s, part_t, nngp, ntk, held, in_sem, out_sem):
    copies = []
    for i in range(2):
        rows = pl.ds(i * 256, 256)
        for j, (src, dst) in enumerate(((part_s, nngp), (part_t, ntk))):
            copies.append(
                (
                    pltpu.make_async_copy(src.at[rows], held.at[i, j], in_sem.at[i, j]),
                    pltpu.make_async_copy(held.at[i, j], dst.at[rows], out_sem.at[i, j]),
                )
            )
    for there, _ in copies:
        there.start()
    for there, back in copies:
        there.wait()
        back.start()
    for _, back in copies:
        back.wait()


def shards(sigma_in, theta_in, var_rows, var_cols, row_nbrs, row_vals, col_nbrs, col_vals):
    smem = pl.BlockSpec(memory_space=pltpu.SMEM)
    hbm = pl.BlockSpec(memory_space=pl.ANY)
    dma = pltpu.SemaphoreType.DMA
    out = jax.ShapeDtypeStruct((512, 1024), F32)
    vmem = pl.BlockSpec(memory_space=pltpu.VMEM)
    var_rows, var_cols = var_rows.reshape(1, 512), var_cols.reshape(1, 1024)
    part_s, part_t = pl.pallas_call(
        kernel,
        out_shape=(out, out),
        in_specs=[hbm, smem, hbm, hbm, hbm, hbm, hbm, hbm],
        out_specs=(hbm, hbm),
        scratch_shapes=[
            pltpu.SMEM((20, 128), jnp.int32),
            pltpu.VMEM((1, 512), F32),
            pltpu.VMEM((1, 1024), F32),
            pltpu.SMEM((64,), jnp.int32),
            pltpu.SMEM((64,), jnp.int32),
            pltpu.SMEM((160,), jnp.int32),
            pltpu.VMEM((80, 256, 256), BF16),
            pltpu.VMEM((6, 256, 256), BF16),
            pltpu.VMEM((8, 256, 1024), BF16),
            pltpu.VMEM((8, 256, 1024), BF16),
            pltpu.VMEM((2, 4, 256, 256), F32),
            pltpu.VMEM((2, 4, 256, 256), F32),
        ]
        + [pltpu.VMEM((5, 4, 128, 256), BF16)] * 8
        + [pltpu.VMEM((4, 128, 256), BF16)] * 8
        + [pltpu.VMEM((SLOTS, 128, 256), BF16)] * 8
        + [pltpu.VMEM((26, 128, 256), BF16)] * 4
        + [
            dma((4,)),
            dma((2,)),
            dma((3, 2, 4)),
            dma((2, 3)),
            dma((2, 3)),
            dma((2, 3)),
            dma((2, 3)),
            dma((4, 2, 5)),
            dma((4, 2, 5)),
            dma((4, 2, 9)),
            dma((4, 2, 9)),
            dma((4, 4)),
            dma((3,)),
        ],
        compiler_params=pltpu.CompilerParams(
            collective_id=0, has_side_effects=True, vmem_limit_bytes=62 * 1024 * 1024
        ),
    )(col_nbrs.T, row_nbrs.T, var_rows, var_cols, theta_in, sigma_in, row_vals, col_vals)

    return pl.pallas_call(
        update,
        out_shape=(out, out),
        in_specs=[hbm, hbm],
        out_specs=(hbm, hbm),
        scratch_shapes=[pltpu.VMEM((2, 2, 256, 1024), F32), dma((2, 2)), dma((2, 2))],
        compiler_params=pltpu.CompilerParams(vmem_limit_bytes=62 * 1024 * 1024),
    )(part_s, part_t)


def solution(mesh):
    in_specs = (
        P("rows", "cols"),
        P("rows", "cols"),
        P("rows"),
        P("cols"),
        P(),
        P(),
        P(),
        P("cols", None, None, None),
    )
    out_specs = (P("rows", "cols"), P("rows", "cols"))
    return jax.shard_map(shards, mesh=mesh, in_specs=in_specs, out_specs=out_specs, check_vma=False)
```
